32 devices in a mesh: grp: 2 (over x), ex: 8 (over z, y), layer: 2 (over core).
Axes of the slice: x: 2, y: 2, z: 4, core: 2. Of those that a mesh axis runs over, the one named last changes fastest.
Arguments:
- acts: bfloat16 [8192, 8, 256], P(('grp', 'ex'), 'layer'), parts along dimension 0, may hold values from -1.5 to 1.5
- grads: bfloat16 [8192, 8, 256], P(('grp', 'ex'), 'layer'), parts along dimension 0, may hold values from -1.5 to 1.5
- adam_scale: float32 [16, 256], P('grp'), parts along dimension 0, may hold values from 0.2 to 5
- plan: int32 [2, 8], replicated, may hold values from 0 to 7, as said below
- assignment: int32 [8], P('layer'), may hold values from 0 to 7, each once
Outputs:
- scores: float32 [2, 8192, 512], P(None, ('grp', 'ex', 'layer')), parts along dimension 1
The draws below stay inside these ranges and needn't reach their ends.
There are 2 independent parts, one for each index of `grp`. The reference program is written for one: setup_inputs(seed, part) draws one part's arguments, and reference() takes and returns one part's arrays. A program takes and returns all parts, laid end to end along the dimension named above; an argument that names none is the same for every part. Nothing has to cross between parts.
Inputs may be any that keep to these rules, and one draw needn't show every extreme that they name: `plan`: in each round the partner of block b is b XOR m for a nonzero m of that round; rounds have different m.
All inputs are finite; a program needn't handle non-finite values.
Results may differ from the reference program's by a relative error of at most 0.0029.
Values may be sent and summed in bfloat16 or wider, within the bound.
No kernel may reach another device: no remote copies, remote signals or barrier semaphores. Data moves between devices by JAX's collectives and lax.ppermute only.
A program may use at most 64 MiB of HBM per device.

```python
import math
import jax
import jax.numpy as jnp
from jax import lax

P_SIZE = 256
BLK = 512
ROUNDS = 2
BLOCKS = 8
MODULES = 8
EXAMPLES = 4096


def draw_plan(key, part):
    masks = jax.random.permutation(key, BLOCKS - 1)[:ROUNDS].astype(jnp.int32) + 1
    blocks = jnp.arange(BLOCKS, dtype=jnp.int32)
    return jnp.bitwise_xor(blocks[None, :], masks[:, None])


def block_levels(own_key, dims, cuts, smallest, top_value):
    level = 1.0
    for axis_at, blocks in cuts:
        draws = jax.random.uniform(jax.random.fold_in(jax.random.fold_in(own_key, 6), axis_at), (blocks,), jnp.float32, smallest / len(cuts), top_value / len(cuts))
        level = level * jnp.repeat(jnp.exp(draws), dims[axis_at] // blocks).reshape((-1,) + (1,) * (len(dims) - 1 - axis_at))
    return level


def scatter_about(stream_key, extent, spread, bound, cuts=(), held_as=jnp.bfloat16):
    entries = spread * jax.random.normal(stream_key, extent, jnp.float32)
    if cuts:
        entries = entries * block_levels(stream_key, extent, cuts, -0.22, 0.18)
    return jnp.clip(entries, -bound, bound).astype(held_as)


def setup_inputs(seed: int = 0, part: int = 0) -> dict:
    seeds = jax.random.split(jax.random.key(seed), 6)
    own_keys = jax.random.split(jax.random.fold_in(seeds[5], part), 6)
    return {
        "acts": scatter_about(own_keys[0], (EXAMPLES, MODULES, P_SIZE), 0.25, 1.5, ((0, 8), (1, 2))),
        "grads": scatter_about(own_keys[1], (EXAMPLES, MODULES, P_SIZE), 0.25, 1.5, ((0, 8), (1, 2))),
        "adam_scale": jnp.clip(jnp.exp(jax.random.uniform(own_keys[2], (MODULES, P_SIZE), jnp.float32, math.log(0.2), math.log(5.0))), 0.2, 5.0),
        "plan": draw_plan(jax.random.fold_in(seeds[5], 71), part),
        "assignment": jax.random.permutation(seeds[4], MODULES).astype(jnp.int32),
    }


def reference(acts, grads, adam_scale, plan, assignment):
    scales = adam_scale[assignment]
    scaled = (grads.astype(jnp.float32) * scales[None]).astype(jnp.bfloat16)
    blocks_act = acts.astype(jnp.float32).reshape(BLOCKS, BLK, MODULES, P_SIZE)
    blocks_scaled = scaled.astype(jnp.float32).reshape(BLOCKS, BLK, MODULES, P_SIZE)
    blocks_grad = grads.astype(jnp.float32).reshape(BLOCKS, BLK, MODULES, P_SIZE)
    results = []
    for round_index in range(ROUNDS):
        partners = plan[round_index]

        def one_block(block_index):
            other = partners[block_index]
            act_gram = jnp.einsum("imp,jmp->mij", blocks_act[block_index], blocks_act[other], precision=lax.Precision.HIGHEST)
            grad_gram = jnp.einsum("imp,jmp->mij", blocks_scaled[block_index], blocks_grad[other], precision=lax.Precision.HIGHEST)
            return jnp.sum(act_gram * grad_gram, axis=0)

        tiles = lax.map(one_block, jnp.arange(BLOCKS, dtype=jnp.int32))
        results.append(tiles.reshape(EXAMPLES, BLK))
    return jnp.stack(results, axis=0)
```

```python
import jax
import jax.numpy as jnp
from jax import lax
from jax.sharding import PartitionSpec as P

CHUNKS = 4
MOST_BLOCKS = 8


def parity(number):
    return bin(number).count("1") & 1


def colouring(low, high, count):
    for vector in range(1, count):
        if parity(vector & low) and parity(vector & high):
            return vector
    return 0


def module_major(rows):
    return jnp.transpose(rows, (1, 0, 2))


def gram_sum(own_acts, own_scaled, partner):
    act_gram = jnp.einsum("mip,mjp->mij", own_acts, partner[0], preferred_element_type=jnp.float32)
    grad_gram = jnp.einsum("mip,mjp->mij", own_scaled, partner[1], preferred_element_type=jnp.float32)
    return jnp.sum(act_gram * grad_gram, axis=0)


def pair_branch(low, high, count):
    vector = colouring(low, high, count)
    feed, aside, same_core, cross_core = [], [], [], []
    for block in range(count):
        for core in range(2):
            here = block * 2 + core
            takes_low = core == parity(block & vector)
            own_mask, other_mask = (low, high) if takes_low else (high, low)
            feed.append((here, (block ^ other_mask) * 2 + core))
            aside.append((here, block * 2 + 1 - core))
            same_core.append((here, (block ^ own_mask) * 2 + core))
            cross_core.append((here, (block ^ own_mask) * 2 + 1 - core))
    axes = ("ex", "layer")

    def branch(chunks, own_acts, own_scaled, core):
        half = own_acts.shape[1] // 2
        received = [lax.ppermute(chunk, axes, feed) for chunk in chunks]
        kept, sent_aside, turned = [], [], []
        for part in received:
            tile = gram_sum(own_acts, own_scaled, part)
            kept.append(lax.dynamic_slice_in_dim(tile, core * half, half, 0))
            sent_aside.append(
                lax.dynamic_slice_in_dim(tile, (1 - core) * half, half, 0).astype(jnp.bfloat16)
            )
            turned.append(tile.T.astype(jnp.bfloat16))
        middle = len(chunks) // 2
        first = jnp.concatenate(turned[:middle], axis=0)
        second = jnp.concatenate(turned[middle:], axis=0)
        from_same = lax.ppermute(first, axes, same_core)
        from_cross = lax.ppermute(second, axes, cross_core)
        from_aside = lax.ppermute(jnp.concatenate(sent_aside, axis=1), axes, aside)
        own = jnp.concatenate(kept, axis=1)
        own = jnp.where(core == 0, own, jnp.roll(own, half, axis=1)) + from_cross.astype(jnp.float32)
        other = jnp.where(core == 1, from_aside, jnp.roll(from_aside, half, axis=1)).astype(
            jnp.float32
        ) + from_same.astype(jnp.float32)
        takes_low = core == (
            sum((lax.axis_index("ex") >> bit) & 1 for bit in range(count.bit_length()) if vector >> bit & 1)
            & 1
        )
        return own, other, takes_low

    return branch


def direct_rounds(acts, grads, own_acts, own_scaled, plan):
    count = lax.axis_size("ex")
    payload = jnp.stack([module_major(acts), module_major(grads)])
    outputs = []
    for round_index in range(plan.shape[0]):
        branches = [
            lambda held, mask=mask: lax.ppermute(
                held, "ex", [(block, block ^ mask) for block in range(count)]
            )
            for mask in range(1, count)
        ]
        received = lax.switch(plan[round_index, 0] - 1, branches, payload)
        tile = gram_sum(own_acts, own_scaled, received)
        outputs.append(lax.psum_scatter(tile, "layer", scatter_dimension=0, tiled=True))
    return jnp.stack(outputs)


def shards(acts, grads, adam_scale, plan, assignment):
    block_rows = acts.shape[0]
    total_modules = adam_scale.shape[0]
    count = lax.axis_size("ex")
    core = lax.axis_index("layer")
    picker = (assignment[:, None] == jnp.arange(total_modules, dtype=jnp.int32)[None, :]).astype(
        jnp.float32
    )
    scales = jnp.dot(picker, adam_scale, precision=lax.Precision.HIGHEST)
    own_acts = module_major(acts)
    own_scaled = (module_major(grads).astype(jnp.float32) * scales[:, None, :]).astype(jnp.bfloat16)
    if count > MOST_BLOCKS:
        return direct_rounds(acts, grads, own_acts, own_scaled, plan)
    half = block_rows // 2
    size = block_rows // CHUNKS
    chunks = []
    for number in range(CHUNKS):
        start = lax.rem(core * half + number * size, block_rows)
        chunks.append(
            jnp.stack(
                [
                    module_major(lax.dynamic_slice_in_dim(whole, start, size, 0))
                    for whole in (acts, grads)
                ]
            )
        )
    first, second = plan[0, 0], plan[1, 0]
    low, high = jnp.minimum(first, second), jnp.maximum(first, second)
    pairs = [(a, b) for b in range(2, count) for a in range(1, b)]
    index = (high - 1) * (high - 2) // 2 + low - 1
    own, other, takes_low = lax.switch(
        index, [pair_branch(a, b, count) for a, b in pairs], chunks, own_acts, own_scaled, core
    )
    own_first = takes_low == (first < second)
    return jnp.stack([jnp.where(own_first, own, other), jnp.where(own_first, other, own)])


def solution(mesh):
    in_specs = (
        P(("grp", "ex"), "layer", None),
        P(("grp", "ex"), "layer", None),
        P("grp", None),
        P(),
        P("layer"),
    )
    out_specs = P(None, ("grp", "ex", "layer"), None)
    return jax.shard_map(shards, mesh=mesh, in_specs=in_specs, out_specs=out_specs, check_vma=False)
```

```python
import jax
import jax.numpy as jnp
from jax import lax
from jax.sharding import PartitionSpec as P

MOST_BLOCKS = 8


def parity(number):
    return bin(number).count("1") & 1


def module_major(rows):
    return jnp.transpose(rows, (1, 0, 2))


def gram_sum(own_acts, own_scaled, partner):
    act_gram = jnp.einsum("mip,mjp->mij", own_acts, partner[0], preferred_element_type=jnp.float32)
    grad_gram = jnp.einsum("mip,mjp->mij", own_scaled, partner[1], preferred_element_type=jnp.float32)
    return jnp.sum(act_gram * grad_gram, axis=0)


def busiest(low, high, vector, count):
    load = {}
    for block in range(count):
        end = block ^ (low if parity(block & vector) else high)
        at, to = block >> 1, end >> 1
        step = 1 if to > at else -1
        while at != to:
            load[at, block & 1, step] = load.get((at, block & 1, step), 0) + 1
            at += step
        if (block ^ end) & 1:
            load[to, block & 1, 0] = load.get((to, block & 1, 0), 0) + 1
    return max(load.values())


def colouring(low, high, count):
    found = [vector for vector in range(1, count) if parity(vector & low) and parity(vector & high)]
    return min(found, key=lambda vector: busiest(low, high, vector, count))


def routes(low, high, count):
    vector = colouring(low, high, count)
    feed, reply = [], []
    for block in range(count):
        own, other = (high, low) if parity(block & vector) else (low, high)
        feed.append((block, block ^ other))
        reply.append((block, block ^ own))
    return feed, reply


def paired_rounds(own_acts, own_grads, own_scaled, plan):
    count = lax.axis_size("ex")
    core = lax.axis_index("layer")
    half = own_acts.shape[1] // 2
    first, second = plan[0, 0], plan[1, 0]
    low, high = jnp.minimum(first, second), jnp.maximum(first, second)
    pairs = [(a, b) for b in range(2, count) for a in range(1, b)]
    index = (high - 1) * (high - 2) // 2 + low - 1
    plans = [routes(a, b, count) for a, b in pairs]
    vectors = jnp.array([colouring(a, b, count) for a, b in pairs], jnp.int32)
    received = lax.switch(
        index,
        [lambda held, feed=feed: lax.ppermute(held, "ex", feed) for feed, _ in plans],
        jnp.stack([own_acts, own_grads]),
    )
    tile = gram_sum(own_acts, own_scaled, received)

    kept = lax.dynamic_slice_in_dim(tile, core * half, half, 0)
    passed = lax.dynamic_slice_in_dim(tile, (1 - core) * half, half, 0)
    corner = lax.dynamic_slice_in_dim(kept, (1 - core) * half, half, 1)
    swap = [(0, 1), (1, 0)]
    across = lax.ppermute(jnp.concatenate([passed, corner], axis=1), "layer", swap)
    own = kept + across[:, : 2 * half]
    same = lax.dynamic_slice_in_dim(own, core * half, half, 1)
    cross = lax.dynamic_slice_in_dim(passed, core * half, half, 1) + across[:, 2 * half :]
    turned = jnp.where(
        core == 0, jnp.concatenate([same, cross], axis=0), jnp.concatenate([cross, same], axis=0)
    ).T.astype(jnp.bfloat16)
    other = lax.switch(
        index,
        [lambda held, reply=reply: lax.ppermute(held, "ex", reply) for _, reply in plans],
        turned,
    ).astype(jnp.float32)

    marked = jnp.bitwise_and(lax.axis_index("ex"), vectors[index])
    colour = lax.population_count(marked) & 1
    own_first = (colour == 0) == (first < second)
    return jnp.stack([jnp.where(own_first, own, other), jnp.where(own_first, other, own)])


def direct_rounds(own_acts, own_grads, own_scaled, plan):
    count = lax.axis_size("ex")
    payload = jnp.stack([own_acts, own_grads])
    outputs = []
    for round_index in range(plan.shape[0]):
        branches = [
            lambda held, mask=mask: lax.ppermute(
                held, "ex", [(block, block ^ mask) for block in range(count)]
            )
            for mask in range(1, count)
        ]
        received = lax.switch(plan[round_index, 0] - 1, branches, payload)
        tile = gram_sum(own_acts, own_scaled, received)
        outputs.append(lax.psum_scatter(tile, "layer", scatter_dimension=0, tiled=True))
    return jnp.stack(outputs)


def shards(acts, grads, adam_scale, plan, assignment):
    total_modules = adam_scale.shape[0]
    count = lax.axis_size("ex")
    picker = (assignment[:, None] == jnp.arange(total_modules, dtype=jnp.int32)[None, :]).astype(
        jnp.float32
    )
    scales = jnp.dot(picker, adam_scale, precision=lax.Precision.HIGHEST)
    own_acts, own_grads = module_major(acts), module_major(grads)
    own_scaled = (own_grads.astype(jnp.float32) * scales[:, None, :]).astype(jnp.bfloat16)
    if count > MOST_BLOCKS:
        return direct_rounds(own_acts, own_grads, own_scaled, plan)
    return paired_rounds(own_acts, own_grads, own_scaled, plan)


def solution(mesh):
    in_specs = (
        P(("grp", "ex"), "layer", None),
        P(("grp", "ex"), "layer", None),
        P("grp", None),
        P(),
        P("layer"),
    )
    out_specs = P(None, ("grp", "ex", "layer"), None)
    return jax.shard_map(shards, mesh=mesh, in_specs=in_specs, out_specs=out_specs, check_vma=False)
```

```python
import functools

import jax
import jax.numpy as jnp
from jax import lax
from jax.experimental import pallas as pl
from jax.experimental.pallas import tpu as pltpu
from jax.sharding import PartitionSpec as P

MOST_BLOCKS = 8
TRANSPOSED = (((1,), (1,)), ((), ()))
VMEM = pl.BlockSpec(memory_space=pltpu.VMEM)
SMEM = pl.BlockSpec(memory_space=pltpu.SMEM)
ROOMY = pltpu.CompilerParams(vmem_limit_bytes=32 * 2**20)


def parity(number):
    return bin(number).count("1") & 1


def module_major(rows):
    return jnp.transpose(rows, (1, 0, 2))


def gram_sum(own_acts, own_scaled, partner):
    act_gram = jnp.einsum("mip,mjp->mij", own_acts, partner[0], preferred_element_type=jnp.float32)
    grad_gram = jnp.einsum("mip,mjp->mij", own_scaled, partner[1], preferred_element_type=jnp.float32)
    return jnp.sum(act_gram * grad_gram, axis=0)


def busiest(low, high, vector, count):
    load = {}
    for block in range(count):
        end = block ^ (low if parity(block & vector) else high)
        at, to = block >> 1, end >> 1
        step = 1 if to > at else -1
        while at != to:
            load[at, block & 1, step] = load.get((at, block & 1, step), 0) + 1
            at += step
        if (block ^ end) & 1:
            load[to, block & 1, 0] = load.get((to, block & 1, 0), 0) + 1
    return max(load.values())


def colouring(low, high, count):
    found = [vector for vector in range(1, count) if parity(vector & low) and parity(vector & high)]
    return min(found, key=lambda vector: busiest(low, high, vector, count))


def routes(low, high, count):
    vector = colouring(low, high, count)
    feed, reply = [], []
    for block in range(count):
        own, other = (high, low) if parity(block & vector) else (low, high)
        feed.append((block, block ^ other))
        reply.append((block, block ^ own))
    return feed, reply


def tile_kernel(core_ref, own, scales, partner, kept, passed):
    core = core_ref[0]
    half, wide = kept.shape

    def grams(row, column):
        total = None
        for module in range(own.shape[1]):
            rows, columns = pl.ds(row, half), pl.ds(column, half)
            act = lax.dot_general(
                own[0, module, rows, :],
                partner[0, module, columns, :],
                TRANSPOSED,
                preferred_element_type=jnp.float32,
            )
            scaled = (
                own[1, module, rows, :].astype(jnp.float32) * scales[module : module + 1, :]
            ).astype(jnp.bfloat16)
            grad = lax.dot_general(
                scaled, partner[1, module, columns, :], TRANSPOSED, preferred_element_type=jnp.float32
            )
            total = act * grad if total is None else total + act * grad
        return total

    mine = pl.multiple_of(core * half, half)
    theirs = pl.multiple_of((1 - core) * half, half)
    for column in range(0, wide, half):
        passed[:, column : column + half] = grams(theirs, column)
        kept[:, column : column + half] = grams(mine, column)
    passed[:, wide:] = kept[:, pl.ds(theirs, half)]


def tile_halves(core, own, scales, partner):
    half = own.shape[2] // 2
    return pl.pallas_call(
        tile_kernel,
        in_specs=[SMEM, VMEM, VMEM, VMEM],
        out_specs=[VMEM, VMEM],
        out_shape=[
            jax.ShapeDtypeStruct((half, 2 * half), jnp.float32),
            jax.ShapeDtypeStruct((half, 3 * half), jnp.float32),
        ],
        compiler_params=ROOMY,
        name="tile",
    )(core, own, scales, partner)


def join_kernel(place, kept, passed, across, out, turned):
    core = place[0]
    half, wide = kept.shape
    out[0] = kept[...] + across[:, :wide]
    mine = pl.ds(pl.multiple_of(core * half, half), half)
    theirs = pl.ds(pl.multiple_of((1 - core) * half, half), half)
    turned[:, mine] = out[0, :, mine].T.astype(turned.dtype)
    turned[:, theirs] = (passed[:, mine] + across[:, wide:]).T.astype(turned.dtype)


def joined(place, kept, passed, across):
    half, wide = kept.shape
    whole = lambda shape: pl.BlockSpec(shape, lambda step, place: (0, 0))
    return pl.pallas_call(
        join_kernel,
        grid_spec=pltpu.PrefetchScalarGridSpec(
            num_scalar_prefetch=1,
            grid=(1,),
            in_specs=[whole(kept.shape), whole(passed.shape), whole(across.shape)],
            out_specs=[
                pl.BlockSpec((1, half, wide), lambda step, place: (place[1], 0, 0)),
                whole((half, wide)),
            ],
        ),
        out_shape=[
            jax.ShapeDtypeStruct((2, half, wide), jnp.float32),
            jax.ShapeDtypeStruct((half, wide), jnp.bfloat16),
        ],
        compiler_params=ROOMY,
        name="join",
    )(place, kept, passed, across)


def fill_kernel(place, reply, held, out):
    out[0] = reply[...].astype(out.dtype)


def filled(place, reply, out):
    half, wide = reply.shape
    return pl.pallas_call(
        fill_kernel,
        grid_spec=pltpu.PrefetchScalarGridSpec(
            num_scalar_prefetch=1,
            grid=(1,),
            in_specs=[
                pl.BlockSpec((half, wide), lambda step, place: (0, 0)),
                pl.BlockSpec(memory_space=pl.ANY),
            ],
            out_specs=pl.BlockSpec((1, half, wide), lambda step, place: (1 - place[1], 0, 0)),
        ),
        out_shape=jax.ShapeDtypeStruct(out.shape, out.dtype),
        input_output_aliases={2: 0},
        compiler_params=ROOMY,
        name="fill",
    )(place, reply, out)


def place_kernel(vectors, plan, index, place):
    first, second = plan[0, 0], plan[1, 0]
    low, high = jnp.minimum(first, second), jnp.maximum(first, second)
    found = jnp.right_shift((high - 1) * (high - 2), 1) + low - 1
    vector = jnp.int32(0)
    for number, choice in enumerate(vectors):
        vector = jnp.where(found == number, jnp.int32(choice), vector)
    marked = jnp.bitwise_and(lax.axis_index("ex"), vector)
    colour = jnp.int32(0)
    for bit in range(max(vectors).bit_length()):
        colour = jnp.bitwise_xor(colour, jnp.bitwise_and(jnp.right_shift(marked, bit), 1))
    index[0] = found
    place[0] = lax.axis_index("layer")
    place[1] = jnp.where(first > second, 1 - colour, colour)


def placed(plan, vectors):
    return pl.pallas_call(
        functools.partial(place_kernel, vectors),
        in_specs=[SMEM],
        out_specs=[SMEM, SMEM],
        out_shape=[jax.ShapeDtypeStruct((1,), jnp.int32), jax.ShapeDtypeStruct((2,), jnp.int32)],
        name="place",
    )(plan)


def paired_rounds(payload, scales, plan):
    count = lax.axis_size("ex")
    pairs = [(a, b) for b in range(2, count) for a in range(1, b)]
    plans = [routes(a, b, count) for a, b in pairs]
    index, place = placed(plan, [colouring(a, b, count) for a, b in pairs])
    index = index[0]
    received = lax.switch(
        index, [lambda held, feed=feed: lax.ppermute(held, "ex", feed) for feed, _ in plans], payload
    )

    kept, passed = tile_halves(place, payload, scales, received)
    across = lax.ppermute(passed, "layer", [(0, 1), (1, 0)])
    out, turned = joined(place, kept, passed, across)
    reply = lax.switch(
        index, [lambda held, reply=reply: lax.ppermute(held, "ex", reply) for _, reply in plans], turned
    )
    return filled(place, reply, out)


def direct_rounds(payload, scales, plan):
    count = lax.axis_size("ex")
    own_scaled = (payload[1].astype(jnp.float32) * scales[:, None, :]).astype(jnp.bfloat16)
    outputs = []
    for round_index in range(plan.shape[0]):
        branches = [
            lambda held, mask=mask: lax.ppermute(
                held, "ex", [(block, block ^ mask) for block in range(count)]
            )
            for mask in range(1, count)
        ]
        received = lax.switch(plan[round_index, 0] - 1, branches, payload)
        tile = gram_sum(payload[0], own_scaled, received)
        outputs.append(lax.psum_scatter(tile, "layer", scatter_dimension=0, tiled=True))
    return jnp.stack(outputs)


def shards(acts, grads, adam_scale, plan, assignment):
    total_modules = adam_scale.shape[0]
    count = lax.axis_size("ex")
    picker = (assignment[:, None] == jnp.arange(total_modules, dtype=jnp.int32)[None, :]).astype(
        jnp.float32
    )
    scales = jnp.dot(picker, adam_scale, precision=lax.Precision.HIGHEST)
    payload = jnp.stack([module_major(acts), module_major(grads)])
    if count > MOST_BLOCKS:
        return direct_rounds(payload, scales, plan)
    return paired_rounds(payload, scales, plan)


def solution(mesh):
    in_specs = (
        P(("grp", "ex"), "layer", None),
        P(("grp", "ex"), "layer", None),
        P("grp", None),
        P(),
        P("layer"),
    )
    out_specs = P(None, ("grp", "ex", "layer"), None)
    return jax.shard_map(shards, mesh=mesh, in_specs=in_specs, out_specs=out_specs, check_vma=False)
```

```python
import functools

import jax
import jax.numpy as jnp
from jax import lax
from jax.experimental import pallas as pl
from jax.experimental.pallas import tpu as pltpu
from jax.sharding import PartitionSpec as P

MOST_BLOCKS = 8
TRANSPOSED = (((1,), (1,)), ((), ()))
VMEM = pl.BlockSpec(memory_space=pltpu.VMEM)
SMEM = pl.BlockSpec(memory_space=pltpu.SMEM)
PIECES = 2
SWAP = [(0, 1), (1, 0)]
ROOMY = pltpu.CompilerParams(vmem_limit_bytes=32 * 2**20)


def parity(number):
    return bin(number).count("1") & 1


def module_major(rows):
    return jnp.transpose(rows, (1, 0, 2))


def gram_sum(own_acts, own_scaled, partner):
    act_gram = jnp.einsum("mip,mjp->mij", own_acts, partner[0], preferred_element_type=jnp.float32)
    grad_gram = jnp.einsum("mip,mjp->mij", own_scaled, partner[1], preferred_element_type=jnp.float32)
    return jnp.sum(act_gram * grad_gram, axis=0)


def busiest(low, high, vector, count):
    load = {}
    for block in range(count):
        end = block ^ (high if parity(block & vector) else low)
        at, to = block >> 1, end >> 1
        step = 1 if to > at else -1
        while at != to:
            load[at, block & 1, step] = load.get((at, block & 1, step), 0) + 1
            at += step
        if (block ^ end) & 1:
            load[to, block & 1, 0] = load.get((to, block & 1, 0), 0) + 1
    return max(load.values())


def colouring(low, high, count):
    found = [vector for vector in range(1, count) if parity(vector & low) and parity(vector & high)]
    return min(found, key=lambda vector: busiest(low, high, vector, count))


def routes(low, high, count):
    vector = colouring(low, high, count)
    feed, reply = [], []
    for block in range(count):
        own, other = (low, high) if parity(block & vector) else (high, low)
        feed.append((block, block ^ other))
        reply.append((block, block ^ own))
    return feed, reply


def tile_halves(core, own, scales, partner, kept, passed):
    half, wide = kept.shape

    def grams(row, column):
        total = None
        for module in range(own.shape[1]):
            rows, columns = pl.ds(row, half), pl.ds(column, half)
            act = lax.dot_general(
                own[0, module, rows, :],
                partner[0, module, columns, :],
                TRANSPOSED,
                preferred_element_type=jnp.float32,
            )
            scaled = (
                own[1, module, rows, :].astype(jnp.float32) * scales[module : module + 1, :]
            ).astype(jnp.bfloat16)
            grad = lax.dot_general(
                scaled, partner[1, module, columns, :], TRANSPOSED, preferred_element_type=jnp.float32
            )
            total = act * grad if total is None else total + act * grad
        return total

    mine = pl.multiple_of(core * half, half)
    theirs = pl.multiple_of((1 - core) * half, half)
    for column in range(0, wide, half):
        passed[:, column : column + half] = grams(theirs, column)
        kept[:, column : column + half] = grams(mine, column)
    passed[:, wide:] = kept[:, pl.ds(theirs, half)]


def tile_kernel(place, own, scales, partner, kept, passed):
    tile_halves(place[0], own, scales, partner, kept, passed)


def two_tiles_kernel(place, own, lent, scales, partner, kept, passed):
    @pl.when(place[2] == 0)
    def _():
        tile_halves(place[0], own, scales, partner, kept.at[0], passed.at[0])
        tile_halves(place[0], lent, scales, partner, kept.at[1], passed.at[1])


def on_device(kernel, shapes, *operands):
    return pl.pallas_call(
        kernel,
        in_specs=[SMEM if operand.ndim == 1 else VMEM for operand in operands],
        out_specs=[VMEM] * len(shapes),
        out_shape=[jax.ShapeDtypeStruct(shape, dtype) for shape, dtype in shapes],
        compiler_params=ROOMY,
        name=kernel.__name__,
    )(*operands)


def join_kernel(place, kept, passed, across, own, turned):
    core = place[0]
    half, wide = kept.shape
    mine = pl.ds(pl.multiple_of(core * half, half), half)
    theirs = pl.ds(pl.multiple_of((1 - core) * half, half), half)
    own[...] = kept[...] + across[:, :wide]
    turned[:, mine] = own[:, mine].T.astype(turned.dtype)
    turned[:, theirs] = (passed[:, mine] + across[:, wide:]).T.astype(turned.dtype)


def write_rows(source, target, held, copies):
    pieces = copies.shape[0]
    size = source.shape[0] // pieces
    started = []
    for piece in range(pieces):
        rows = pl.ds(piece * size, size)
        if source.dtype != held.dtype:
            held[rows, :] = source[rows, :].astype(held.dtype)
        copy = pltpu.make_async_copy(
            (source if source.dtype == held.dtype else held).at[rows, :],
            target.at[rows, :],
            copies.at[piece],
        )
        copy.start()
        started.append(copy)
    return started


def fill_kernel(place, own, reply, out, held, copies):
    started = write_rows(own, out.at[place[1]], held.at[0], copies.at[0])
    started += write_rows(reply, out.at[1 - place[1]], held.at[1], copies.at[1])
    for copy in started:
        copy.wait()


def settle_kernel(place, own, lent, turned, out, held, copies):
    @pl.when(place[2] == 0)
    def _():
        fill_kernel(place, own, lent, out, held, copies)

    @pl.when(place[2] == 1)
    def _():
        fill_kernel(place, turned.at[0], turned.at[1], out, held, copies)


def settled(kernel, place, *operands):
    half, wide = operands[0].shape
    return pl.pallas_call(
        kernel,
        in_specs=[SMEM] + [VMEM] * len(operands),
        out_specs=pl.BlockSpec(memory_space=pltpu.HBM),
        out_shape=pltpu.HBM((2, half, wide), jnp.float32),
        scratch_shapes=[
            pltpu.VMEM((2, half, wide), jnp.float32),
            pltpu.SemaphoreType.DMA((2, PIECES)),
        ],
        compiler_params=ROOMY,
        name=kernel.__name__,
    )(place, *operands)


def join_two_kernel(place, kept, passed, across, own, lent, turned):
    @pl.when(place[2] == 0)
    def _():
        core = place[0]
        half, wide = own.shape
        mine = pl.ds(pl.multiple_of(core * half, half), half)
        theirs = pl.ds(pl.multiple_of((1 - core) * half, half), half)
        own[...] = kept[0] + across[0, :, :wide]
        lent[...] = (kept[1] + across[1, :, :wide]).astype(lent.dtype)
        for number in range(2):
            turned[number, :, mine] = (
                (kept[number, :, mine] + across[number, :, mine]).T.astype(turned.dtype)
            )
            turned[number, :, theirs] = (
                (passed[number, :, mine] + across[number, :, wide:]).T.astype(turned.dtype)
            )


def place_kernel(table, plan, model, scale_table, index, place, scales):
    first, second = plan[0, 0], plan[1, 0]
    low, high = jnp.minimum(first, second), jnp.maximum(first, second)
    found = jnp.right_shift((high - 1) * (high - 2), 1) + low - 1
    picked = [jnp.int32(0)] * len(table[0])
    for number, row in enumerate(table):
        picked = [
            jnp.where(found == number, jnp.int32(value), held) for value, held in zip(row, picked)
        ]
    vector, branch, by_colour, turned_over = picked
    marked = jnp.bitwise_and(lax.axis_index("ex"), vector)
    colour = jnp.int32(0)
    for bit in range(max(row[0] for row in table).bit_length()):
        colour = jnp.bitwise_xor(colour, jnp.bitwise_and(jnp.right_shift(marked, bit), 1))
    slot = jnp.bitwise_xor(jnp.bitwise_and(colour, by_colour), turned_over)
    index[0] = branch
    place[0] = lax.axis_index("layer")
    place[1] = jnp.where(first > second, 1 - slot, slot)
    place[2] = colour
    for module in range(model.shape[0]):
        scales[module : module + 1, :] = scale_table[pl.ds(model[module], 1), :]


def placed(table, plan, model, scale_table):
    return pl.pallas_call(
        functools.partial(place_kernel, table),
        in_specs=[SMEM, SMEM, VMEM],
        out_specs=[SMEM, SMEM, VMEM],
        out_shape=[
            jax.ShapeDtypeStruct((1,), jnp.int32),
            jax.ShapeDtypeStruct((3,), jnp.int32),
            jax.ShapeDtypeStruct((model.shape[0], scale_table.shape[1]), jnp.float32),
        ],
        name="place",
    )(plan, model, scale_table)


def permuted(operand, route):
    return lax.ppermute(operand, "ex", route)


def apart(plans, index, place, payload, scales):
    half = payload.shape[2] // 2
    received = lax.switch(
        index, [lambda held, feed=feed: permuted(held, feed) for feed, _ in plans], payload
    )
    kept, passed = on_device(
        tile_kernel,
        [((half, 2 * half), jnp.float32), ((half, 3 * half), jnp.float32)],
        place,
        payload,
        scales,
        received,
    )
    across = lax.ppermute(passed, "layer", SWAP)
    own, turned = on_device(
        join_kernel,
        [((half, 2 * half), jnp.float32), ((half, 2 * half), jnp.bfloat16)],
        place,
        kept,
        passed,
        across,
    )
    reply = lax.switch(
        index, [lambda held, reply=reply: permuted(held, reply) for _, reply in plans], turned
    )
    return settled(fill_kernel, place, own, reply)


def crossed_routes(mask, between, vector, count):
    feed = [(block, block ^ mask) for block in range(count) if parity(block & vector)]
    lend = [(block, block ^ between) for block in range(count) if not parity(block & vector)]
    reply = [(block, block ^ mask) for block in range(count) if not parity(block & vector)]
    return feed, lend, reply


def together(plans, index, place, payload, scales):
    half = payload.shape[2] // 2
    received, lent = lax.switch(
        index,
        [
            lambda held, feed=feed, lend=lend: (permuted(held, feed), permuted(held, lend))
            for feed, lend, _ in plans
        ],
        payload,
    )
    kept, passed = on_device(
        two_tiles_kernel,
        [((2, half, 2 * half), jnp.float32), ((2, half, 3 * half), jnp.float32)],
        place,
        payload,
        lent,
        scales,
        received,
    )
    across = lax.ppermute(passed, "layer", SWAP)
    own, rows, turned = on_device(
        join_two_kernel,
        [
            ((half, 2 * half), jnp.float32),
            ((half, 2 * half), jnp.bfloat16),
            ((2, half, 2 * half), jnp.bfloat16),
        ],
        place,
        kept,
        passed,
        across,
    )
    turned, rows = lax.switch(
        index,
        [
            lambda held, rows, lend=lend, reply=reply: (permuted(held, reply), permuted(rows, lend))
            for _, lend, reply in plans
        ],
        turned,
        rows,
    )
    return settled(settle_kernel, place, own, rows, turned)


def paired_rounds(payload, scale_table, plan, model):
    count = lax.axis_size("ex")
    top = count // 2
    apart_plans, together_plans, table = [], [], []
    for high in range(2, count):
        for low in range(1, high):
            vector = colouring(low, high, count)
            if low >= top and (low ^ high) & 1:
                mask = high if low & 1 else low
                vector = next(
                    choice
                    for choice in range(count - 1, 0, -1)
                    if parity(choice & low) and parity(choice & high) and choice & 2
                )
                table.append((vector, len(together_plans), 0, int(mask == high)))
                together_plans.append(crossed_routes(mask, low ^ high, vector, count))
            else:
                table.append((vector, len(apart_plans), 1, 1))
                apart_plans.append(routes(low, high, count))
    table = [
        (row[0], row[1] + len(apart_plans) * (1 - row[2]), row[2], row[3]) for row in table
    ]
    index, place, scales = placed(table, plan, model, scale_table)
    branch = index[0]
    return lax.cond(
        branch < len(apart_plans),
        functools.partial(apart, apart_plans),
        lambda branch, *operands: together(together_plans, branch - len(apart_plans), *operands),
        branch,
        place,
        payload,
        scales,
    )


def direct_rounds(payload, scales, plan):
    count = lax.axis_size("ex")
    own_scaled = (payload[1].astype(jnp.float32) * scales[:, None, :]).astype(jnp.bfloat16)
    outputs = []
    for round_index in range(plan.shape[0]):
        branches = [
            lambda held, mask=mask: lax.ppermute(
                held, "ex", [(block, block ^ mask) for block in range(count)]
            )
            for mask in range(1, count)
        ]
        received = lax.switch(plan[round_index, 0] - 1, branches, payload)
        tile = gram_sum(payload[0], own_scaled, received)
        outputs.append(lax.psum_scatter(tile, "layer", scatter_dimension=0, tiled=True))
    return jnp.stack(outputs)


def shards(acts, grads, adam_scale, plan, assignment):
    count = lax.axis_size("ex")
    payload = jnp.stack([module_major(acts), module_major(grads)])
    if count > MOST_BLOCKS:
        return direct_rounds(payload, adam_scale[assignment], plan)
    return paired_rounds(payload, adam_scale, plan, assignment)


def solution(mesh):
    in_specs = (
        P(("grp", "ex"), "layer", None),
        P(("grp", "ex"), "layer", None),
        P("grp", None),
        P(),
        P("layer"),
    )
    out_specs = P(None, ("grp", "ex", "layer"), None)
    return jax.shard_map(shards, mesh=mesh, in_specs=in_specs, out_specs=out_specs, check_vma=False)
```

```python
import functools

import jax
import jax.numpy as jnp
from jax import lax
from jax.experimental import pallas as pl
from jax.experimental.pallas import tpu as pltpu
from jax.sharding import PartitionSpec as P

MOST_BLOCKS = 8
TRANSPOSED = (((1,), (1,)), ((), ()))
VMEM = pl.BlockSpec(memory_space=pltpu.VMEM)
SMEM = pl.BlockSpec(memory_space=pltpu.SMEM)
PIECES = 2
SWAP = [(0, 1), (1, 0)]
ROOMY = pltpu.CompilerParams(vmem_limit_bytes=32 * 2**20)


def parity(number):
    return bin(number).count("1") & 1


def module_major(rows):
    return jnp.transpose(rows, (1, 0, 2))


def gram_sum(own_acts, own_scaled, partner):
    act_gram = jnp.einsum("mip,mjp->mij", own_acts, partner[0], preferred_element_type=jnp.float32)
    grad_gram = jnp.einsum("mip,mjp->mij", own_scaled, partner[1], preferred_element_type=jnp.float32)
    return jnp.sum(act_gram * grad_gram, axis=0)


def busiest(low, high, vector, count):
    load = {}
    for block in range(count):
        end = block ^ (high if parity(block & vector) else low)
        at, to = block >> 1, end >> 1
        step = 1 if to > at else -1
        while at != to:
            load[at, block & 1, step] = load.get((at, block & 1, step), 0) + 1
            at += step
        if (block ^ end) & 1:
            load[to, block & 1, 0] = load.get((to, block & 1, 0), 0) + 1
    return max(load.values())


def colouring(low, high, count):
    found = [vector for vector in range(1, count) if parity(vector & low) and parity(vector & high)]
    return min(found, key=lambda vector: busiest(low, high, vector, count))


def routes(low, high, count):
    vector = colouring(low, high, count)
    feed, reply = [], []
    for block in range(count):
        own, other = (low, high) if parity(block & vector) else (high, low)
        feed.append((block, block ^ other))
        reply.append((block, block ^ own))
    return feed, reply


def grams(own, scales, partner, row, column, size):
    total = None
    for module in range(own.shape[1]):
        rows, columns = pl.ds(row, size), pl.ds(column, size)
        act = lax.dot_general(
            own[0, module, rows, :],
            partner[0, module, columns, :],
            TRANSPOSED,
            preferred_element_type=jnp.float32,
        )
        scaled = (
            own[1, module, rows, :].astype(jnp.float32) * scales[module : module + 1, :]
        ).astype(jnp.bfloat16)
        grad = lax.dot_general(
            scaled, partner[1, module, columns, :], TRANSPOSED, preferred_element_type=jnp.float32
        )
        total = act * grad if total is None else total + act * grad
    return total


def parts_of(core, half):
    return pl.multiple_of(core * half, half), pl.multiple_of((1 - core) * half, half)


def tile_halves(core, own, scales, partner, kept, passed):
    half, wide = kept.shape
    mine, theirs = parts_of(core, half)
    for column in range(0, wide, half):
        passed[:, column : column + half] = grams(own, scales, partner, theirs, column, half)
        kept[:, column : column + half] = grams(own, scales, partner, mine, column, half)
    passed[:, wide:] = kept[:, pl.ds(theirs, half)]


def tile_kernel(place, own, scales, partner, kept, passed):
    tile_halves(place[0], own, scales, partner, kept, passed)


def two_tiles_kernel(place, own, lent, scales, partner, kept, passed):
    @pl.when(place[2] == 0)
    def _():
        tile_halves(place[0], own, scales, partner, kept.at[0], passed.at[0])
        tile_halves(place[0], lent, scales, partner, kept.at[1], passed.at[1])


def on_device(kernel, shapes, *operands):
    return pl.pallas_call(
        kernel,
        in_specs=[SMEM if operand.ndim == 1 else VMEM for operand in operands],
        out_specs=[VMEM] * len(shapes),
        out_shape=[jax.ShapeDtypeStruct(shape, dtype) for shape, dtype in shapes],
        compiler_params=ROOMY,
        name=kernel.__name__,
    )(*operands)


def join_kernel(place, kept, passed, across, own, turned):
    core = place[0]
    half, wide = kept.shape
    mine = pl.ds(pl.multiple_of(core * half, half), half)
    theirs = pl.ds(pl.multiple_of((1 - core) * half, half), half)
    own[...] = kept[...] + across[:, :wide]
    turned[:, mine] = own[:, mine].T.astype(turned.dtype)
    turned[:, theirs] = (passed[:, mine] + across[:, wide:]).T.astype(turned.dtype)


def write_rows(source, target, held, copies):
    pieces = copies.shape[0]
    size = source.shape[0] // pieces
    started = []
    for piece in range(pieces):
        rows = pl.ds(piece * size, size)
        if source.dtype != held.dtype:
            held[rows, :] = source[rows, :].astype(held.dtype)
        copy = pltpu.make_async_copy(
            (source if source.dtype == held.dtype else held).at[rows, :],
            target.at[rows, :],
            copies.at[piece],
        )
        copy.start()
        started.append(copy)
    return started


def fill_kernel(place, own, reply, out, held, copies):
    started = write_rows(own, out.at[place[1]], held.at[0], copies.at[0])
    started += write_rows(reply, out.at[1 - place[1]], held.at[1], copies.at[1])
    for copy in started:
        copy.wait()


def settle_kernel(place, own, lent, turned, out, held, copies):
    @pl.when(place[2] == 0)
    def _():
        fill_kernel(place, own, lent, out, held, copies)

    @pl.when(place[2] == 1)
    def _():
        fill_kernel(place, turned.at[0], turned.at[1], out, held, copies)


def settled(kernel, place, *operands):
    half, wide = operands[0].shape
    return pl.pallas_call(
        kernel,
        in_specs=[SMEM] + [VMEM] * len(operands),
        out_specs=pl.BlockSpec(memory_space=pltpu.HBM),
        out_shape=pltpu.HBM((2, half, wide), jnp.float32),
        scratch_shapes=[
            pltpu.VMEM((2, half, wide), jnp.float32),
            pltpu.SemaphoreType.DMA((2, PIECES)),
        ],
        compiler_params=ROOMY,
        name=kernel.__name__,
    )(place, *operands)


def join_two_kernel(place, kept, passed, across, own, lent, turned):
    @pl.when(place[2] == 0)
    def _():
        core = place[0]
        half, wide = own.shape
        mine = pl.ds(pl.multiple_of(core * half, half), half)
        theirs = pl.ds(pl.multiple_of((1 - core) * half, half), half)
        own[...] = kept[0] + across[0, :, :wide]
        lent[...] = (kept[1] + across[1, :, :wide]).astype(lent.dtype)
        for number in range(2):
            turned[number, :, mine] = (
                (kept[number, :, mine] + across[number, :, mine]).T.astype(turned.dtype)
            )
            turned[number, :, theirs] = (
                (passed[number, :, mine] + across[number, :, wide:]).T.astype(turned.dtype)
            )


def quarters_kernel(place, own, lent, scales, partner, kept, passed, kept_turned, passed_turned):
    @pl.when(place[2] == 0)
    def _():
        half = kept.shape[1]
        mine, theirs = parts_of(place[0], half)
        for number, rows in enumerate((own, lent)):
            for row, by_row in ((theirs, passed), (mine, kept)):
                for column, by_column in ((theirs, passed_turned), (mine, kept_turned)):
                    square = grams(rows, scales, partner, row, column, half)
                    by_row[number, :, pl.ds(column, half)] = square
                    by_column[number, :, pl.ds(row, half)] = square.T.astype(by_column.dtype)


def choose_kernel(place, kept, across, kept_turned, across_turned, own, lent, turned):
    for colour, rows, columns in ((0, kept, kept_turned), (1, across, across_turned)):

        @pl.when(place[2] == colour)
        def _(rows=rows, columns=columns):
            own[...] = rows[0]
            lent[...] = rows[1]
            turned[...] = columns[...]


def add_kernel(place, own, lent, turned, out, held, copies):
    started = []
    for number, (rows, slot) in enumerate(((own, place[1]), (lent, 1 - place[1]))):
        held[number] = rows[...] + turned[number].astype(held.dtype)
        started += write_rows(held.at[number], out.at[slot], held.at[number], copies.at[number])
    for copy in started:
        copy.wait()


def place_kernel(table, plan, model, scale_table, index, place, scales):
    first, second = plan[0, 0], plan[1, 0]
    low, high = jnp.minimum(first, second), jnp.maximum(first, second)
    found = jnp.right_shift((high - 1) * (high - 2), 1) + low - 1
    picked = [jnp.int32(0)] * len(table[0])
    for number, row in enumerate(table):
        picked = [
            jnp.where(found == number, jnp.int32(value), held) for value, held in zip(row, picked)
        ]
    vector, branch, by_colour, turned_over, by_core = picked
    marked = jnp.bitwise_and(lax.axis_index("ex"), vector)
    core = lax.axis_index("layer")
    colour = jnp.bitwise_and(core, by_core)
    for bit in range(max(row[0] for row in table).bit_length()):
        colour = jnp.bitwise_xor(colour, jnp.bitwise_and(jnp.right_shift(marked, bit), 1))
    slot = jnp.bitwise_xor(jnp.bitwise_and(colour, by_colour), turned_over)
    index[0] = branch
    place[0] = core
    place[1] = jnp.where(first > second, 1 - slot, slot)
    place[2] = colour
    for module in range(model.shape[0]):
        scales[module : module + 1, :] = scale_table[pl.ds(model[module], 1), :]


def placed(table, plan, model, scale_table):
    return pl.pallas_call(
        functools.partial(place_kernel, table),
        in_specs=[SMEM, SMEM, VMEM],
        out_specs=[SMEM, SMEM, VMEM],
        out_shape=[
            jax.ShapeDtypeStruct((1,), jnp.int32),
            jax.ShapeDtypeStruct((3,), jnp.int32),
            jax.ShapeDtypeStruct((model.shape[0], scale_table.shape[1]), jnp.float32),
        ],
        name="place",
    )(plan, model, scale_table)


def permuted(operand, route):
    return lax.ppermute(operand, "ex", route)


def apart(plans, index, place, payload, scales):
    half = payload.shape[2] // 2
    received = lax.switch(
        index, [lambda held, feed=feed: permuted(held, feed) for feed, _ in plans], payload
    )
    kept, passed = on_device(
        tile_kernel,
        [((half, 2 * half), jnp.float32), ((half, 3 * half), jnp.float32)],
        place,
        payload,
        scales,
        received,
    )
    across = lax.ppermute(passed, "layer", SWAP)
    own, turned = on_device(
        join_kernel,
        [((half, 2 * half), jnp.float32), ((half, 2 * half), jnp.bfloat16)],
        place,
        kept,
        passed,
        across,
    )
    reply = lax.switch(
        index, [lambda held, reply=reply: permuted(held, reply) for _, reply in plans], turned
    )
    return settled(fill_kernel, place, own, reply)


def crossed_routes(mask, between, vector, count):
    feed = [(block, block ^ mask) for block in range(count) if parity(block & vector)]
    lend = [(block, block ^ between) for block in range(count) if not parity(block & vector)]
    reply = [(block, block ^ mask) for block in range(count) if not parity(block & vector)]
    return feed, lend, reply


def together(plans, index, place, payload, scales):
    half = payload.shape[2] // 2
    received, lent = lax.switch(
        index,
        [
            lambda held, feed=feed, lend=lend: (permuted(held, feed), permuted(held, lend))
            for feed, lend, _ in plans
        ],
        payload,
    )
    kept, passed = on_device(
        two_tiles_kernel,
        [((2, half, 2 * half), jnp.float32), ((2, half, 3 * half), jnp.float32)],
        place,
        payload,
        lent,
        scales,
        received,
    )
    across = lax.ppermute(passed, "layer", SWAP)
    own, rows, turned = on_device(
        join_two_kernel,
        [
            ((half, 2 * half), jnp.float32),
            ((half, 2 * half), jnp.bfloat16),
            ((2, half, 2 * half), jnp.bfloat16),
        ],
        place,
        kept,
        passed,
        across,
    )
    turned, rows = lax.switch(
        index,
        [
            lambda held, rows, lend=lend, reply=reply: (permuted(held, reply), permuted(rows, lend))
            for _, lend, reply in plans
        ],
        turned,
        rows,
    )
    return settled(settle_kernel, place, own, rows, turned)


def split_routes(mask, between, vector, count):
    feed, lend = [], []
    for block in range(count):
        for core in range(2):
            lends = parity(block & vector) == core
            end = block ^ (between if lends else mask)
            (lend if lends else feed).append((block * 2 + core, end * 2 + core))
    reply, back = ([(block, block ^ way) for block in range(count)] for way in (mask, between))
    return feed, lend, reply, back


def split(plans, index, place, payload, scales):
    half = payload.shape[2] // 2
    axes = ("ex", "layer")
    received, lent = lax.switch(
        index,
        [
            lambda held, feed=feed, lend=lend: (
                lax.ppermute(held, axes, feed),
                lax.ppermute(held, axes, lend),
            )
            for feed, lend, _, _ in plans
        ],
        payload,
    )
    shape = (2, half, 2 * half)
    kept, passed, kept_turned, passed_turned = on_device(
        quarters_kernel,
        [(shape, jnp.float32)] * 2 + [(shape, jnp.bfloat16)] * 2,
        place,
        payload,
        lent,
        scales,
        received,
    )
    across = lax.ppermute(passed, "layer", SWAP)
    across_turned = lax.ppermute(passed_turned, "layer", SWAP)
    own, rows, turned = on_device(
        choose_kernel,
        [(shape[1:], jnp.float32)] * 2 + [(shape, jnp.bfloat16)],
        place,
        kept,
        across,
        kept_turned,
        across_turned,
    )
    turned, rows = lax.switch(
        index,
        [
            lambda held, rows, reply=reply, back=back: (permuted(held, reply), permuted(rows, back))
            for _, _, reply, back in plans
        ],
        turned,
        rows,
    )
    return settled(add_kernel, place, own, rows, turned)


def paired_rounds(payload, scale_table, plan, model):
    count = lax.axis_size("ex")
    top = count // 2
    apart_plans, together_plans, split_plans, table = [], [], [], []
    for high in range(2, count):
        for low in range(1, high):
            if low < top:
                vector = colouring(low, high, count)
                table.append((vector, (0, len(apart_plans)), 1, 1, 0))
                apart_plans.append(routes(low, high, count))
                continue
            mask = high if low & 1 else low
            turned_over = int(mask == high)
            if (low ^ high) & 1:
                vector = next(
                    choice
                    for choice in range(count - 1, 0, -1)
                    if parity(choice & low) and parity(choice & high) and choice & 2
                )
                table.append((vector, (1, len(together_plans)), 0, turned_over, 0))
                together_plans.append(crossed_routes(mask, low ^ high, vector, count))
            else:
                table.append((top, (2, len(split_plans)), 0, turned_over, 1))
                split_plans.append(split_routes(mask, low ^ high, top, count))
    kinds = [
        (way, plans)
        for way, plans in ((apart, apart_plans), (together, together_plans), (split, split_plans))
    ]
    starts = [sum(len(plans) for _, plans in kinds[:kind]) for kind in range(len(kinds))]
    table = [(row[0], starts[row[1][0]] + row[1][1], *row[2:]) for row in table]
    branch, place, scales = placed(table, plan, model, scale_table)
    branch = branch[0]
    kind = sum((branch >= start).astype(jnp.int32) for start in starts[1:])
    return lax.switch(
        kind,
        [
            lambda branch, *operands, way=way, plans=plans, start=start: way(
                plans, branch - start, *operands
            )
            for (way, plans), start in zip(kinds, starts)
        ],
        branch,
        place,
        payload,
        scales,
    )


def direct_rounds(payload, scales, plan):
    count = lax.axis_size("ex")
    own_scaled = (payload[1].astype(jnp.float32) * scales[:, None, :]).astype(jnp.bfloat16)
    outputs = []
    for round_index in range(plan.shape[0]):
        branches = [
            lambda held, mask=mask: lax.ppermute(
                held, "ex", [(block, block ^ mask) for block in range(count)]
            )
            for mask in range(1, count)
        ]
        received = lax.switch(plan[round_index, 0] - 1, branches, payload)
        tile = gram_sum(payload[0], own_scaled, received)
        outputs.append(lax.psum_scatter(tile, "layer", scatter_dimension=0, tiled=True))
    return jnp.stack(outputs)


def shards(acts, grads, adam_scale, plan, assignment):
    count = lax.axis_size("ex")
    payload = jnp.stack([module_major(acts), module_major(grads)])
    if count > MOST_BLOCKS:
        return direct_rounds(payload, adam_scale[assignment], plan)
    return paired_rounds(payload, adam_scale, plan, assignment)


def solution(mesh):
    in_specs = (
        P(("grp", "ex"), "layer", None),
        P(("grp", "ex"), "layer", None),
        P("grp", None),
        P(),
        P("layer"),
    )
    out_specs = P(None, ("grp", "ex", "layer"), None)
    return jax.shard_map(shards, mesh=mesh, in_specs=in_specs, out_specs=out_specs, check_vma=False)
```

```python
import functools

import jax
import jax.numpy as jnp
from jax import lax
from jax.experimental import pallas as pl
from jax.experimental.pallas import tpu as pltpu
from jax.sharding import PartitionSpec as P

MOST_BLOCKS = 8
TRANSPOSED = (((1,), (1,)), ((), ()))
VMEM = pl.BlockSpec(memory_space=pltpu.VMEM)
SMEM = pl.BlockSpec(memory_space=pltpu.SMEM)
PIECES = 2
READ_PARTS = 4
SWAP = [(0, 1), (1, 0)]
FULL = pltpu.CompilerParams(vmem_limit_bytes=123 * 2**19)
ROOMY = pltpu.CompilerParams(vmem_limit_bytes=32 * 2**20)


def parity(number):
    return bin(number).count("1") & 1


def module_major(rows):
    return jnp.transpose(rows, (1, 0, 2))


def gram_sum(own_acts, own_scaled, partner):
    act_gram = jnp.einsum("mip,mjp->mij", own_acts, partner[0], preferred_element_type=jnp.float32)
    grad_gram = jnp.einsum("mip,mjp->mij", own_scaled, partner[1], preferred_element_type=jnp.float32)
    return jnp.sum(act_gram * grad_gram, axis=0)


def busiest(low, high, vector, count):
    load = {}
    for block in range(count):
        end = block ^ (high if parity(block & vector) else low)
        at, to = block >> 1, end >> 1
        step = 1 if to > at else -1
        while at != to:
            load[at, block & 1, step] = load.get((at, block & 1, step), 0) + 1
            at += step
        if (block ^ end) & 1:
            load[to, block & 1, 0] = load.get((to, block & 1, 0), 0) + 1
    return max(load.values())


def colouring(low, high, count):
    found = [vector for vector in range(1, count) if parity(vector & low) and parity(vector & high)]
    return min(found, key=lambda vector: busiest(low, high, vector, count))


def routes(low, high, count):
    vector = colouring(low, high, count)
    feed, reply = [], []
    for block in range(count):
        own, other = (low, high) if parity(block & vector) else (high, low)
        feed.append((block, block ^ other))
        reply.append((block, block ^ own))
    return feed, reply


def grams(own, scales, partner, row, column, size):
    total = None
    for module in range(own.shape[1]):
        rows, columns = pl.ds(row, size), pl.ds(column, size)
        act = lax.dot_general(
            own[0, module, rows, :],
            partner[0, module, columns, :],
            TRANSPOSED,
            preferred_element_type=jnp.float32,
        )
        scaled = (
            own[1, module, rows, :].astype(jnp.float32) * scales[module : module + 1, :]
        ).astype(jnp.bfloat16)
        grad = lax.dot_general(
            scaled, partner[1, module, columns, :], TRANSPOSED, preferred_element_type=jnp.float32
        )
        total = act * grad if total is None else total + act * grad
    return total


def parts_of(core, half):
    return pl.multiple_of(core * half, half), pl.multiple_of((1 - core) * half, half)


def tile_halves(core, own, scales, partner, kept, passed):
    half, wide = kept.shape
    mine, theirs = parts_of(core, half)
    for column in range(0, wide, half):
        passed[:, column : column + half] = grams(own, scales, partner, theirs, column, half)
        kept[:, column : column + half] = grams(own, scales, partner, mine, column, half)
    passed[:, wide:] = kept[:, pl.ds(theirs, half)]


def tile_kernel(place, own, scales, partner, kept, passed):
    tile_halves(place[0], own, scales, partner, kept, passed)


def two_tiles_kernel(place, own, lent, scales, partner, kept, passed):
    @pl.when(place[2] == 0)
    def _():
        tile_halves(place[0], own, scales, partner, kept.at[0], passed.at[0])
        tile_halves(place[0], lent, scales, partner, kept.at[1], passed.at[1])


def on_device(kernel, shapes, *operands):
    return pl.pallas_call(
        kernel,
        in_specs=[SMEM if operand.ndim == 1 else VMEM for operand in operands],
        out_specs=[VMEM] * len(shapes),
        out_shape=[jax.ShapeDtypeStruct(shape, dtype) for shape, dtype in shapes],
        compiler_params=ROOMY,
        name=kernel.__name__,
    )(*operands)


def join_kernel(place, kept, passed, across, own, turned):
    core = place[0]
    half, wide = kept.shape
    mine = pl.ds(pl.multiple_of(core * half, half), half)
    theirs = pl.ds(pl.multiple_of((1 - core) * half, half), half)
    own[...] = kept[...] + across[:, :wide]
    turned[:, mine] = own[:, mine].T.astype(turned.dtype)
    turned[:, theirs] = (passed[:, mine] + across[:, wide:]).T.astype(turned.dtype)


def write_rows(source, target, held, copies):
    pieces = copies.shape[0]
    size = source.shape[0] // pieces
    started = []
    for piece in range(pieces):
        rows = pl.ds(piece * size, size)
        if source.dtype != held.dtype:
            held[rows, :] = source[rows, :].astype(held.dtype)
        copy = pltpu.make_async_copy(
            (source if source.dtype == held.dtype else held).at[rows, :],
            target.at[rows, :],
            copies.at[piece],
        )
        copy.start()
        started.append(copy)
    return started


def fill_kernel(place, own, reply, out, held, copies):
    started = write_rows(own, out.at[place[1]], held.at[0], copies.at[0])
    started += write_rows(reply, out.at[1 - place[1]], held.at[1], copies.at[1])
    for copy in started:
        copy.wait()


def settle_kernel(place, own, lent, turned, out, held, copies):
    @pl.when(place[2] == 0)
    def _():
        fill_kernel(place, own, lent, out, held, copies)

    @pl.when(place[2] == 1)
    def _():
        fill_kernel(place, turned.at[0], turned.at[1], out, held, copies)


def settled(kernel, place, *operands):
    half, wide = operands[0].shape
    return pl.pallas_call(
        kernel,
        in_specs=[SMEM] + [VMEM] * len(operands),
        out_specs=pl.BlockSpec(memory_space=pltpu.HBM),
        out_shape=pltpu.HBM((2, half, wide), jnp.float32),
        scratch_shapes=[
            pltpu.VMEM((2, half, wide), jnp.float32),
            pltpu.SemaphoreType.DMA((2, PIECES)),
        ],
        compiler_params=ROOMY,
        name=kernel.__name__,
    )(place, *operands)


def join_two_kernel(place, kept, passed, across, own, lent, turned):
    @pl.when(place[2] == 0)
    def _():
        core = place[0]
        half, wide = own.shape
        mine = pl.ds(pl.multiple_of(core * half, half), half)
        theirs = pl.ds(pl.multiple_of((1 - core) * half, half), half)
        own[...] = kept[0] + across[0, :, :wide]
        lent[...] = (kept[1] + across[1, :, :wide]).astype(lent.dtype)
        for number in range(2):
            turned[number, :, mine] = (
                (kept[number, :, mine] + across[number, :, mine]).T.astype(turned.dtype)
            )
            turned[number, :, theirs] = (
                (passed[number, :, mine] + across[number, :, wide:]).T.astype(turned.dtype)
            )


def quarters_kernel(place, own, lent, scales, partner, kept, passed, kept_turned, passed_turned):
    @pl.when(place[2] == 0)
    def _():
        half = kept.shape[1]
        mine, theirs = parts_of(place[0], half)
        for number, rows in enumerate((own, lent)):
            for row, by_row in ((theirs, passed), (mine, kept)):
                for column, by_column in ((theirs, passed_turned), (mine, kept_turned)):
                    square = grams(rows, scales, partner, row, column, half)
                    by_row[number, :, pl.ds(column, half)] = square
                    by_column[number, :, pl.ds(row, half)] = square.T.astype(by_column.dtype)


def choose_kernel(place, kept, across, kept_turned, across_turned, own, lent, turned):
    for colour, rows, columns in ((0, kept, kept_turned), (1, across, across_turned)):

        @pl.when(place[2] == colour)
        def _(rows=rows, columns=columns):
            own[...] = rows[0]
            lent[...] = rows[1]
            turned[...] = columns[...]


def add_kernel(place, own, lent, turned, out, held, copies):
    started = []
    for number, (rows, slot) in enumerate(((own, place[1]), (lent, 1 - place[1]))):
        held[number] = rows[...] + turned[number].astype(held.dtype)
        started += write_rows(held.at[number], out.at[slot], held.at[number], copies.at[number])
    for copy in started:
        copy.wait()


def place_kernel(
    table, plan, model, scale_table, acts, grads, kind, index, place, scales, payload, held, copies
):
    parts = copies.shape[1]
    size = acts.shape[0] // parts
    pieces = []
    for part in range(parts):
        rows = pl.ds(part * size, size)
        for number, whole in enumerate((acts, grads)):
            copy = pltpu.make_async_copy(whole.at[rows], held.at[number, rows], copies.at[number, part])
            copy.start()
            pieces.append((number, rows, copy))
    first, second = plan[0, 0], plan[1, 0]
    low, high = jnp.minimum(first, second), jnp.maximum(first, second)
    found = jnp.right_shift((high - 1) * (high - 2), 1) + low - 1
    picked = [jnp.int32(0)] * len(table[0])
    for number, row in enumerate(table):
        picked = [
            jnp.where(found == number, jnp.int32(value), held) for value, held in zip(row, picked)
        ]
    vector, way, branch, by_colour, turned_over, by_core = picked
    marked = jnp.bitwise_and(lax.axis_index("ex"), vector)
    core = lax.axis_index("layer")
    colour = jnp.bitwise_and(core, by_core)
    for bit in range(max(row[0] for row in table).bit_length()):
        colour = jnp.bitwise_xor(colour, jnp.bitwise_and(jnp.right_shift(marked, bit), 1))
    slot = jnp.bitwise_xor(jnp.bitwise_and(colour, by_colour), turned_over)
    kind[0] = way
    index[0] = branch
    place[0] = core
    place[1] = jnp.where(first > second, 1 - slot, slot)
    place[2] = colour
    for module in range(model.shape[0]):
        scales[module : module + 1, :] = scale_table[pl.ds(model[module], 1), :]
    for number, rows, copy in pieces:
        copy.wait()
        payload[number, :, rows, :] = jnp.swapaxes(held[number, rows], 0, 1)


def placed(table, plan, model, scale_table, acts, grads):
    rows, modules, width = acts.shape
    return pl.pallas_call(
        functools.partial(place_kernel, table),
        in_specs=[SMEM, SMEM, VMEM] + [pl.BlockSpec(memory_space=pltpu.HBM)] * 2,
        out_specs=[SMEM, SMEM, SMEM, VMEM, VMEM],
        out_shape=[
            jax.ShapeDtypeStruct((1,), jnp.int32),
            jax.ShapeDtypeStruct((1,), jnp.int32),
            jax.ShapeDtypeStruct((3,), jnp.int32),
            jax.ShapeDtypeStruct((modules, width), jnp.float32),
            jax.ShapeDtypeStruct((2, modules, rows, width), acts.dtype),
        ],
        scratch_shapes=[
            pltpu.VMEM((2, rows, modules, width), acts.dtype),
            pltpu.SemaphoreType.DMA((2, READ_PARTS)),
        ],
        compiler_params=FULL,
        name="place",
    )(plan, model, scale_table, acts, grads)


def permuted(operand, route):
    return lax.ppermute(operand, "ex", route)


def apart(plans, index, place, payload, scales):
    half = payload.shape[2] // 2
    received = lax.switch(
        index, [lambda held, feed=feed: permuted(held, feed) for feed, _ in plans], payload
    )
    kept, passed = on_device(
        tile_kernel,
        [((half, 2 * half), jnp.float32), ((half, 3 * half), jnp.float32)],
        place,
        payload,
        scales,
        received,
    )
    across = lax.ppermute(passed, "layer", SWAP)
    own, turned = on_device(
        join_kernel,
        [((half, 2 * half), jnp.float32), ((half, 2 * half), jnp.bfloat16)],
        place,
        kept,
        passed,
        across,
    )
    reply = lax.switch(
        index, [lambda held, reply=reply: permuted(held, reply) for _, reply in plans], turned
    )
    return settled(fill_kernel, place, own, reply)


def crossed_routes(mask, between, vector, count):
    feed = [(block, block ^ mask) for block in range(count) if parity(block & vector)]
    lend = [(block, block ^ between) for block in range(count) if not parity(block & vector)]
    reply = [(block, block ^ mask) for block in range(count) if not parity(block & vector)]
    return feed, lend, reply


def together(plans, index, place, payload, scales):
    half = payload.shape[2] // 2
    received, lent = lax.switch(
        index,
        [
            lambda held, feed=feed, lend=lend: (permuted(held, feed), permuted(held, lend))
            for feed, lend, _ in plans
        ],
        payload,
    )
    kept, passed = on_device(
        two_tiles_kernel,
        [((2, half, 2 * half), jnp.float32), ((2, half, 3 * half), jnp.float32)],
        place,
        payload,
        lent,
        scales,
        received,
    )
    across = lax.ppermute(passed, "layer", SWAP)
    own, rows, turned = on_device(
        join_two_kernel,
        [
            ((half, 2 * half), jnp.float32),
            ((half, 2 * half), jnp.bfloat16),
            ((2, half, 2 * half), jnp.bfloat16),
        ],
        place,
        kept,
        passed,
        across,
    )
    turned, rows = lax.switch(
        index,
        [
            lambda held, rows, lend=lend, reply=reply: (permuted(held, reply), permuted(rows, lend))
            for _, lend, reply in plans
        ],
        turned,
        rows,
    )
    return settled(settle_kernel, place, own, rows, turned)


def split_routes(mask, between, vector, count):
    feed, lend = [], []
    for block in range(count):
        for core in range(2):
            lends = parity(block & vector) == core
            end = block ^ (between if lends else mask)
            (lend if lends else feed).append((block * 2 + core, end * 2 + core))
    reply, back = ([(block, block ^ way) for block in range(count)] for way in (mask, between))
    return feed, lend, reply, back


def split(plans, index, place, payload, scales):
    half = payload.shape[2] // 2
    axes = ("ex", "layer")
    received, lent = lax.switch(
        index,
        [
            lambda held, feed=feed, lend=lend: (
                lax.ppermute(held, axes, feed),
                lax.ppermute(held, axes, lend),
            )
            for feed, lend, _, _ in plans
        ],
        payload,
    )
    shape = (2, half, 2 * half)
    kept, passed, kept_turned, passed_turned = on_device(
        quarters_kernel,
        [(shape, jnp.float32)] * 2 + [(shape, jnp.bfloat16)] * 2,
        place,
        payload,
        lent,
        scales,
        received,
    )
    across = lax.ppermute(passed, "layer", SWAP)
    across_turned = lax.ppermute(passed_turned, "layer", SWAP)
    own, rows, turned = on_device(
        choose_kernel,
        [(shape[1:], jnp.float32)] * 2 + [(shape, jnp.bfloat16)],
        place,
        kept,
        across,
        kept_turned,
        across_turned,
    )
    turned, rows = lax.switch(
        index,
        [
            lambda held, rows, reply=reply, back=back: (permuted(held, reply), permuted(rows, back))
            for _, _, reply, back in plans
        ],
        turned,
        rows,
    )
    return settled(add_kernel, place, own, rows, turned)


def paired_rounds(acts, grads, scale_table, plan, model):
    count = lax.axis_size("ex")
    top = count // 2
    apart_plans, together_plans, split_plans, table = [], [], [], []
    for high in range(2, count):
        for low in range(1, high):
            shared = low & high
            if shared == 0 or high >= top > low:
                vector = colouring(low, high, count)
                table.append((vector, 0, len(apart_plans), 1, 1, 0))
                apart_plans.append(routes(low, high, count))
                continue
            mask = low if high < top or not low & 1 else high
            turned_over = int(mask == high)
            if low >= top and (low ^ high) & 1:
                vector = next(
                    choice
                    for choice in range(count - 1, 0, -1)
                    if parity(choice & low) and parity(choice & high) and choice & 2
                )
                table.append((vector, 1, len(together_plans), 0, turned_over, 0))
                together_plans.append(crossed_routes(mask, low ^ high, vector, count))
            else:
                side = top if low >= top else 1 << shared.bit_length() - 1
                table.append((side, 2, len(split_plans), 0, turned_over, 1))
                split_plans.append(split_routes(mask, low ^ high, side, count))
    kind, index, place, scales, payload = placed(table, plan, model, scale_table, acts, grads)
    ways = ((apart, apart_plans), (together, together_plans), (split, split_plans))
    return lax.switch(
        kind[0],
        [functools.partial(way, plans) for way, plans in ways],
        index[0],
        place,
        payload,
        scales,
    )


def direct_rounds(acts, grads, scales, plan):
    count = lax.axis_size("ex")
    payload = jnp.stack([module_major(acts), module_major(grads)])
    own_scaled = (payload[1].astype(jnp.float32) * scales[:, None, :]).astype(jnp.bfloat16)
    outputs = []
    for round_index in range(plan.shape[0]):
        branches = [
            lambda held, mask=mask: lax.ppermute(
                held, "ex", [(block, block ^ mask) for block in range(count)]
            )
            for mask in range(1, count)
        ]
        received = lax.switch(plan[round_index, 0] - 1, branches, payload)
        tile = gram_sum(payload[0], own_scaled, received)
        outputs.append(lax.psum_scatter(tile, "layer", scatter_dimension=0, tiled=True))
    return jnp.stack(outputs)


def shards(acts, grads, adam_scale, plan, assignment):
    if lax.axis_size("ex") > MOST_BLOCKS:
        return direct_rounds(acts, grads, adam_scale[assignment], plan)
    return paired_rounds(acts, grads, adam_scale, plan, assignment)


def solution(mesh):
    in_specs = (
        P(("grp", "ex"), "layer", None),
        P(("grp", "ex"), "layer", None),
        P("grp", None),
        P(),
        P("layer"),
    )
    out_specs = P(None, ("grp", "ex", "layer"), None)
    return jax.shard_map(shards, mesh=mesh, in_specs=in_specs, out_specs=out_specs, check_vma=False)
```

```python
import functools

import jax
import jax.numpy as jnp
from jax import lax
from jax.experimental import pallas as pl
from jax.experimental.pallas import tpu as pltpu
from jax.sharding import PartitionSpec as P

MOST_BLOCKS = 8
TRANSPOSED = (((1,), (1,)), ((), ()))
VMEM = pl.BlockSpec(memory_space=pltpu.VMEM)
SMEM = pl.BlockSpec(memory_space=pltpu.SMEM)
PIECES = 2
SWAP = [(0, 1), (1, 0)]
ROOMY = pltpu.CompilerParams(vmem_limit_bytes=32 * 2**20)


def parity(number):
    return bin(number).count("1") & 1


def module_major(rows):
    return jnp.transpose(rows, (1, 0, 2))


def gram_sum(own_acts, own_scaled, partner):
    act_gram = jnp.einsum("mip,mjp->mij", own_acts, partner[0], preferred_element_type=jnp.float32)
    grad_gram = jnp.einsum("mip,mjp->mij", own_scaled, partner[1], preferred_element_type=jnp.float32)
    return jnp.sum(act_gram * grad_gram, axis=0)


def busiest(low, high, vector, count):
    load = {}
    for block in range(count):
        end = block ^ (high if parity(block & vector) else low)
        at, to = block >> 1, end >> 1
        step = 1 if to > at else -1
        while at != to:
            load[at, block & 1, step] = load.get((at, block & 1, step), 0) + 1
            at += step
        if (block ^ end) & 1:
            load[to, block & 1, 0] = load.get((to, block & 1, 0), 0) + 1
    return max(load.values())


def colouring(low, high, count):
    found = [vector for vector in range(1, count) if parity(vector & low) and parity(vector & high)]
    return min(found, key=lambda vector: busiest(low, high, vector, count))


def routes(low, high, count):
    vector = colouring(low, high, count)
    feed, reply = [], []
    for block in range(count):
        own, other = (low, high) if parity(block & vector) else (high, low)
        feed.append((block, block ^ other))
        reply.append((block, block ^ own))
    return feed, reply


def grams(own, scales, partner, row, column, size):
    total = None
    for module in range(own.shape[1]):
        rows, columns = pl.ds(row, size), pl.ds(column, size)
        act = lax.dot_general(
            own[0, module, rows, :],
            partner[0, module, columns, :],
            TRANSPOSED,
            preferred_element_type=jnp.float32,
        )
        scaled = (
            own[1, module, rows, :].astype(jnp.float32) * scales[module : module + 1, :]
        ).astype(jnp.bfloat16)
        grad = lax.dot_general(
            scaled, partner[1, module, columns, :], TRANSPOSED, preferred_element_type=jnp.float32
        )
        total = act * grad if total is None else total + act * grad
    return total


def parts_of(core, half):
    return pl.multiple_of(core * half, half), pl.multiple_of((1 - core) * half, half)


def tile_halves(core, own, scales, partner, kept, passed):
    half, wide = kept.shape
    mine, theirs = parts_of(core, half)
    for column in range(0, wide, half):
        passed[:, column : column + half] = grams(own, scales, partner, theirs, column, half)
        kept[:, column : column + half] = grams(own, scales, partner, mine, column, half)
    passed[:, wide:] = kept[:, pl.ds(theirs, half)]


def tile_kernel(place, own, scales, partner, kept, passed):
    tile_halves(place[0], own, scales, partner, kept, passed)


def two_tiles_kernel(place, own, lent, scales, partner, kept, passed):
    @pl.when(place[2] == 0)
    def _():
        tile_halves(place[0], own, scales, partner, kept.at[0], passed.at[0])
        tile_halves(place[0], lent, scales, partner, kept.at[1], passed.at[1])


def on_device(kernel, shapes, *operands):
    return pl.pallas_call(
        kernel,
        in_specs=[SMEM if operand.ndim == 1 else VMEM for operand in operands],
        out_specs=[VMEM] * len(shapes),
        out_shape=[jax.ShapeDtypeStruct(shape, dtype) for shape, dtype in shapes],
        compiler_params=ROOMY,
        name=kernel.__name__,
    )(*operands)


def join_kernel(place, kept, passed, across, own, turned):
    core = place[0]
    half, wide = kept.shape
    mine = pl.ds(pl.multiple_of(core * half, half), half)
    theirs = pl.ds(pl.multiple_of((1 - core) * half, half), half)
    own[...] = kept[...] + across[:, :wide]
    turned[:, mine] = own[:, mine].T.astype(turned.dtype)
    turned[:, theirs] = (passed[:, mine] + across[:, wide:]).T.astype(turned.dtype)


def write_rows(source, target, held, copies):
    pieces = copies.shape[0]
    size = source.shape[0] // pieces
    started = []
    for piece in range(pieces):
        rows = pl.ds(piece * size, size)
        if source.dtype != held.dtype:
            held[rows, :] = source[rows, :].astype(held.dtype)
        copy = pltpu.make_async_copy(
            (source if source.dtype == held.dtype else held).at[rows, :],
            target.at[rows, :],
            copies.at[piece],
        )
        copy.start()
        started.append(copy)
    return started


def fill_kernel(place, own, reply, out, held, copies):
    started = write_rows(own, out.at[place[1]], held.at[0], copies.at[0])
    started += write_rows(reply, out.at[1 - place[1]], held.at[1], copies.at[1])
    for copy in started:
        copy.wait()


def settle_kernel(place, own, lent, turned, out, held, copies):
    @pl.when(place[2] == 0)
    def _():
        fill_kernel(place, own, lent, out, held, copies)

    @pl.when(place[2] == 1)
    def _():
        fill_kernel(place, turned.at[0], turned.at[1], out, held, copies)


def settled(kernel, place, *operands):
    half, wide = operands[0].shape
    return pl.pallas_call(
        kernel,
        in_specs=[SMEM] + [VMEM] * len(operands),
        out_specs=pl.BlockSpec(memory_space=pltpu.HBM),
        out_shape=pltpu.HBM((2, half, wide), jnp.float32),
        scratch_shapes=[
            pltpu.VMEM((2, half, wide), jnp.float32),
            pltpu.SemaphoreType.DMA((2, PIECES)),
        ],
        compiler_params=ROOMY,
        name=kernel.__name__,
    )(place, *operands)


def join_two_kernel(place, kept, passed, across, own, lent, turned):
    @pl.when(place[2] == 0)
    def _():
        core = place[0]
        half, wide = own.shape
        mine = pl.ds(pl.multiple_of(core * half, half), half)
        theirs = pl.ds(pl.multiple_of((1 - core) * half, half), half)
        own[...] = kept[0] + across[0, :, :wide]
        lent[...] = (kept[1] + across[1, :, :wide]).astype(lent.dtype)
        for number in range(2):
            turned[number, :, mine] = (
                (kept[number, :, mine] + across[number, :, mine]).T.astype(turned.dtype)
            )
            turned[number, :, theirs] = (
                (passed[number, :, mine] + across[number, :, wide:]).T.astype(turned.dtype)
            )


def quarters_kernel(place, own, lent, scales, partner, kept, passed, kept_turned, passed_turned):
    @pl.when(place[2] == 0)
    def _():
        half = kept.shape[1]
        mine, theirs = parts_of(place[0], half)
        for number, rows in enumerate((own, lent)):
            for row, by_row in ((theirs, passed), (mine, kept)):
                for column, by_column in ((theirs, passed_turned), (mine, kept_turned)):
                    square = grams(rows, scales, partner, row, column, half)
                    by_row[number, :, pl.ds(column, half)] = square
                    by_column[number, :, pl.ds(row, half)] = square.T.astype(by_column.dtype)


def choose_kernel(place, kept, across, kept_turned, across_turned, own, lent, turned):
    for colour, rows, columns in ((0, kept, kept_turned), (1, across, across_turned)):

        @pl.when(place[2] == colour)
        def _(rows=rows, columns=columns):
            own[...] = rows[0]
            lent[...] = rows[1]
            turned[...] = columns[...]


def add_kernel(place, own, lent, turned, out, held, copies):
    started = []
    for number, (rows, slot) in enumerate(((own, place[1]), (lent, 1 - place[1]))):
        held[number] = rows[...] + turned[number].astype(held.dtype)
        started += write_rows(held.at[number], out.at[slot], held.at[number], copies.at[number])
    for copy in started:
        copy.wait()


def place_kernel(table, plan, model, scale_table, kind, index, place, scales):
    first, second = plan[0, 0], plan[1, 0]
    low, high = jnp.minimum(first, second), jnp.maximum(first, second)
    found = jnp.right_shift((high - 1) * (high - 2), 1) + low - 1
    picked = [jnp.int32(0)] * len(table[0])
    for number, row in enumerate(table):
        picked = [
            jnp.where(found == number, jnp.int32(value), held) for value, held in zip(row, picked)
        ]
    vector, way, branch, by_colour, turned_over, by_core = picked
    marked = jnp.bitwise_and(lax.axis_index("ex"), vector)
    core = lax.axis_index("layer")
    colour = jnp.bitwise_and(core, by_core)
    for bit in range(max(row[0] for row in table).bit_length()):
        colour = jnp.bitwise_xor(colour, jnp.bitwise_and(jnp.right_shift(marked, bit), 1))
    slot = jnp.bitwise_xor(jnp.bitwise_and(colour, by_colour), turned_over)
    kind[0] = way
    index[0] = branch
    place[0] = core
    place[1] = jnp.where(first > second, 1 - slot, slot)
    place[2] = colour
    for module in range(model.shape[0]):
        scales[module : module + 1, :] = scale_table[pl.ds(model[module], 1), :]


def placed(table, plan, model, scale_table):
    return pl.pallas_call(
        functools.partial(place_kernel, table),
        in_specs=[SMEM, SMEM, VMEM],
        out_specs=[SMEM, SMEM, SMEM, VMEM],
        out_shape=[
            jax.ShapeDtypeStruct((1,), jnp.int32),
            jax.ShapeDtypeStruct((1,), jnp.int32),
            jax.ShapeDtypeStruct((3,), jnp.int32),
            jax.ShapeDtypeStruct((model.shape[0], scale_table.shape[1]), jnp.float32),
        ],
        name="place",
    )(plan, model, scale_table)


def permuted(operand, route):
    return lax.ppermute(operand, "ex", route)


def apart(plans, index, place, payload, scales):
    half = payload.shape[2] // 2
    received = lax.switch(
        index, [lambda held, feed=feed: permuted(held, feed) for feed, _ in plans], payload
    )
    kept, passed = on_device(
        tile_kernel,
        [((half, 2 * half), jnp.float32), ((half, 3 * half), jnp.float32)],
        place,
        payload,
        scales,
        received,
    )
    across = lax.ppermute(passed, "layer", SWAP)
    own, turned = on_device(
        join_kernel,
        [((half, 2 * half), jnp.float32), ((half, 2 * half), jnp.bfloat16)],
        place,
        kept,
        passed,
        across,
    )
    reply = lax.switch(
        index, [lambda held, reply=reply: permuted(held, reply) for _, reply in plans], turned
    )
    return settled(fill_kernel, place, own, reply)


def crossed_routes(mask, between, vector, count):
    feed = [(block, block ^ mask) for block in range(count) if parity(block & vector)]
    lend = [(block, block ^ between) for block in range(count) if not parity(block & vector)]
    reply = [(block, block ^ mask) for block in range(count) if not parity(block & vector)]
    return feed, lend, reply


def together(plans, index, place, payload, scales):
    half = payload.shape[2] // 2
    received, lent = lax.switch(
        index,
        [
            lambda held, feed=feed, lend=lend: (permuted(held, feed), permuted(held, lend))
            for feed, lend, _ in plans
        ],
        payload,
    )
    kept, passed = on_device(
        two_tiles_kernel,
        [((2, half, 2 * half), jnp.float32), ((2, half, 3 * half), jnp.float32)],
        place,
        payload,
        lent,
        scales,
        received,
    )
    across = lax.ppermute(passed, "layer", SWAP)
    own, rows, turned = on_device(
        join_two_kernel,
        [
            ((half, 2 * half), jnp.float32),
            ((half, 2 * half), jnp.bfloat16),
            ((2, half, 2 * half), jnp.bfloat16),
        ],
        place,
        kept,
        passed,
        across,
    )
    turned, rows = lax.switch(
        index,
        [
            lambda held, rows, lend=lend, reply=reply: (permuted(held, reply), permuted(rows, lend))
            for _, lend, reply in plans
        ],
        turned,
        rows,
    )
    return settled(settle_kernel, place, own, rows, turned)


def split_routes(mask, between, vector, count):
    feed, lend = [], []
    for block in range(count):
        for core in range(2):
            lends = parity(block & vector) == core
            end = block ^ (between if lends else mask)
            (lend if lends else feed).append((block * 2 + core, end * 2 + core))
    reply, back = ([(block, block ^ way) for block in range(count)] for way in (mask, between))
    return feed, lend, reply, back


def split(plans, index, place, payload, scales):
    half = payload.shape[2] // 2
    axes = ("ex", "layer")
    received, lent = lax.switch(
        index,
        [
            lambda held, feed=feed, lend=lend: (
                lax.ppermute(held, axes, feed),
                lax.ppermute(held, axes, lend),
            )
            for feed, lend, _, _ in plans
        ],
        payload,
    )
    shape = (2, half, 2 * half)
    kept, passed, kept_turned, passed_turned = on_device(
        quarters_kernel,
        [(shape, jnp.float32)] * 2 + [(shape, jnp.bfloat16)] * 2,
        place,
        payload,
        lent,
        scales,
        received,
    )
    across = lax.ppermute(passed, "layer", SWAP)
    across_turned = lax.ppermute(passed_turned, "layer", SWAP)
    own, rows, turned = on_device(
        choose_kernel,
        [(shape[1:], jnp.float32)] * 2 + [(shape, jnp.bfloat16)],
        place,
        kept,
        across,
        kept_turned,
        across_turned,
    )
    turned, rows = lax.switch(
        index,
        [
            lambda held, rows, reply=reply, back=back: (permuted(held, reply), permuted(rows, back))
            for _, _, reply, back in plans
        ],
        turned,
        rows,
    )
    return settled(add_kernel, place, own, rows, turned)


def paired_rounds(payload, scale_table, plan, model):
    count = lax.axis_size("ex")
    top = count // 2
    apart_plans, together_plans, split_plans, table = [], [], [], []
    for high in range(2, count):
        for low in range(1, high):
            shared = low & high
            if shared == 0 or high >= top > low:
                vector = colouring(low, high, count)
                table.append((vector, 0, len(apart_plans), 1, 1, 0))
                apart_plans.append(routes(low, high, count))
                continue
            mask = low if high < top or not low & 1 else high
            turned_over = int(mask == high)
            if low >= top and (low ^ high) & 1:
                vector = next(
                    choice
                    for choice in range(count - 1, 0, -1)
                    if parity(choice & low) and parity(choice & high) and choice & 2
                )
                table.append((vector, 1, len(together_plans), 0, turned_over, 0))
                together_plans.append(crossed_routes(mask, low ^ high, vector, count))
            else:
                side = top if low >= top else 1 << shared.bit_length() - 1
                table.append((side, 2, len(split_plans), 0, turned_over, 1))
                split_plans.append(split_routes(mask, low ^ high, side, count))
    kind, index, place, scales = placed(table, plan, model, scale_table)
    ways = ((apart, apart_plans), (together, together_plans), (split, split_plans))
    return lax.switch(
        kind[0],
        [functools.partial(way, plans) for way, plans in ways],
        index[0],
        place,
        payload,
        scales,
    )


def direct_rounds(payload, scales, plan):
    count = lax.axis_size("ex")
    own_scaled = (payload[1].astype(jnp.float32) * scales[:, None, :]).astype(jnp.bfloat16)
    outputs = []
    for round_index in range(plan.shape[0]):
        branches = [
            lambda held, mask=mask: lax.ppermute(
                held, "ex", [(block, block ^ mask) for block in range(count)]
            )
            for mask in range(1, count)
        ]
        received = lax.switch(plan[round_index, 0] - 1, branches, payload)
        tile = gram_sum(payload[0], own_scaled, received)
        outputs.append(lax.psum_scatter(tile, "layer", scatter_dimension=0, tiled=True))
    return jnp.stack(outputs)


def shards(acts, grads, adam_scale, plan, assignment):
    payload = jnp.stack([module_major(acts), module_major(grads)])
    if lax.axis_size("ex") > MOST_BLOCKS:
        return direct_rounds(payload, adam_scale[assignment], plan)
    return paired_rounds(payload, adam_scale, plan, assignment)


def solution(mesh):
    in_specs = (
        P(("grp", "ex"), "layer", None),
        P(("grp", "ex"), "layer", None),
        P("grp", None),
        P(),
        P("layer"),
    )
    out_specs = P(None, ("grp", "ex", "layer"), None)
    return jax.shard_map(shards, mesh=mesh, in_specs=in_specs, out_specs=out_specs, check_vma=False)
```

```python
import functools

import jax
import jax.numpy as jnp
from jax import lax
from jax.experimental import pallas as pl
from jax.experimental.pallas import tpu as pltpu
from jax.sharding import PartitionSpec as P

MOST_BLOCKS = 8
TRANSPOSED = (((1,), (1,)), ((), ()))
VMEM = pl.BlockSpec(memory_space=pltpu.VMEM)
SMEM = pl.BlockSpec(memory_space=pltpu.SMEM)
PIECES = 2
SWAP = [(0, 1), (1, 0)]
ROOMY = pltpu.CompilerParams(vmem_limit_bytes=32 * 2**20)


def parity(number):
    return bin(number).count("1") & 1


def module_major(rows):
    return jnp.transpose(rows, (1, 0, 2))


def gram_sum(own_acts, own_scaled, partner):
    act_gram = jnp.einsum("mip,mjp->mij", own_acts, partner[0], preferred_element_type=jnp.float32)
    grad_gram = jnp.einsum("mip,mjp->mij", own_scaled, partner[1], preferred_element_type=jnp.float32)
    return jnp.sum(act_gram * grad_gram, axis=0)


def busiest(low, high, vector, count):
    load = {}
    for block in range(count):
        end = block ^ (high if parity(block & vector) else low)
        at, to = block >> 1, end >> 1
        step = 1 if to > at else -1
        while at != to:
            load[at, block & 1, step] = load.get((at, block & 1, step), 0) + 1
            at += step
        if (block ^ end) & 1:
            load[to, block & 1, 0] = load.get((to, block & 1, 0), 0) + 1
    return max(load.values())


def colouring(low, high, count):
    found = [vector for vector in range(1, count) if parity(vector & low) and parity(vector & high)]
    return min(found, key=lambda vector: busiest(low, high, vector, count))


def routes(low, high, count):
    vector = colouring(low, high, count)
    feed, reply = [], []
    for block in range(count):
        own, other = (low, high) if parity(block & vector) else (high, low)
        feed.append((block, block ^ other))
        reply.append((block, block ^ own))
    return feed, reply


def grams(own, scales, partner, row, column, size):
    total = None
    for module in range(own.shape[1]):
        rows, columns = pl.ds(row, size), pl.ds(column, size)
        act = lax.dot_general(
            own[0, module, rows, :],
            partner[0, module, columns, :],
            TRANSPOSED,
            preferred_element_type=jnp.float32,
        )
        scaled = (
            own[1, module, rows, :].astype(jnp.float32) * scales[module : module + 1, :]
        ).astype(jnp.bfloat16)
        grad = lax.dot_general(
            scaled, partner[1, module, columns, :], TRANSPOSED, preferred_element_type=jnp.float32
        )
        total = act * grad if total is None else total + act * grad
    return total


def parts_of(core, half):
    return pl.multiple_of(core * half, half), pl.multiple_of((1 - core) * half, half)


def tile_halves(core, own, scales, partner, kept, passed):
    half, wide = kept.shape
    mine, theirs = parts_of(core, half)
    for column in range(0, wide, half):
        passed[:, column : column + half] = grams(own, scales, partner, theirs, column, half)
        kept[:, column : column + half] = grams(own, scales, partner, mine, column, half)
    passed[:, wide:] = kept[:, pl.ds(theirs, half)]


def tile_kernel(place, own, scales, partner, kept, passed):
    tile_halves(place[0], own, scales, partner, kept, passed)


def two_tiles_kernel(place, own, lent, scales, partner, kept, passed):
    @pl.when(place[2] == 0)
    def _():
        tile_halves(place[0], own, scales, partner, kept.at[0], passed.at[0])
        tile_halves(place[0], lent, scales, partner, kept.at[1], passed.at[1])


def on_device(kernel, shapes, *operands):
    return pl.pallas_call(
        kernel,
        in_specs=[SMEM if operand.ndim == 1 else VMEM for operand in operands],
        out_specs=[VMEM] * len(shapes),
        out_shape=[jax.ShapeDtypeStruct(shape, dtype) for shape, dtype in shapes],
        compiler_params=ROOMY,
        name=kernel.__name__,
    )(*operands)


def join_kernel(place, kept, passed, across, own, turned):
    core = place[0]
    half, wide = kept.shape
    mine = pl.ds(pl.multiple_of(core * half, half), half)
    theirs = pl.ds(pl.multiple_of((1 - core) * half, half), half)
    own[...] = kept[...] + across[:, :wide]
    turned[:, mine] = own[:, mine].T.astype(turned.dtype)
    turned[:, theirs] = (passed[:, mine] + across[:, wide:]).T.astype(turned.dtype)


def write_rows(source, target, held, copies):
    pieces = copies.shape[0]
    size = source.shape[0] // pieces
    started = []
    for piece in range(pieces):
        rows = pl.ds(piece * size, size)
        if source.dtype != held.dtype:
            held[rows, :] = source[rows, :].astype(held.dtype)
        copy = pltpu.make_async_copy(
            (source if source.dtype == held.dtype else held).at[rows, :],
            target.at[rows, :],
            copies.at[piece],
        )
        copy.start()
        started.append(copy)
    return started


def fill_kernel(place, own, reply, out, held, copies):
    started = write_rows(own, out.at[place[1]], held.at[0], copies.at[0])
    started += write_rows(reply, out.at[1 - place[1]], held.at[1], copies.at[1])
    for copy in started:
        copy.wait()


def settle_kernel(place, own, lent, turned, out, held, copies):
    @pl.when(place[2] == 0)
    def _():
        fill_kernel(place, own, lent, out, held, copies)

    @pl.when(place[2] == 1)
    def _():
        fill_kernel(place, turned.at[0], turned.at[1], out, held, copies)


def settled(kernel, place, *operands):
    half, wide = operands[0].shape
    return pl.pallas_call(
        kernel,
        in_specs=[SMEM] + [VMEM] * len(operands),
        out_specs=pl.BlockSpec(memory_space=pltpu.HBM),
        out_shape=pltpu.HBM((2, half, wide), jnp.float32),
        scratch_shapes=[
            pltpu.VMEM((2, half, wide), jnp.float32),
            pltpu.SemaphoreType.DMA((2, PIECES)),
        ],
        compiler_params=ROOMY,
        name=kernel.__name__,
    )(place, *operands)


def join_two_kernel(place, kept, passed, across, own, lent, turned):
    @pl.when(place[2] == 0)
    def _():
        core = place[0]
        half, wide = own.shape
        mine = pl.ds(pl.multiple_of(core * half, half), half)
        theirs = pl.ds(pl.multiple_of((1 - core) * half, half), half)
        own[...] = kept[0] + across[0, :, :wide]
        lent[...] = (kept[1] + across[1, :, :wide]).astype(lent.dtype)
        for number in range(2):
            turned[number, :, mine] = (
                (kept[number, :, mine] + across[number, :, mine]).T.astype(turned.dtype)
            )
            turned[number, :, theirs] = (
                (passed[number, :, mine] + across[number, :, wide:]).T.astype(turned.dtype)
            )


def quarters_kernel(place, own, lent, scales, partner, kept, passed, kept_turned, passed_turned):
    @pl.when(place[2] == 0)
    def _():
        half = kept.shape[1]
        mine, theirs = parts_of(place[0], half)
        for number, rows in enumerate((own, lent)):
            for row, by_row in ((theirs, passed), (mine, kept)):
                for column, by_column in ((theirs, passed_turned), (mine, kept_turned)):
                    square = grams(rows, scales, partner, row, column, half)
                    by_row[number, :, pl.ds(column, half)] = square
                    by_column[number, :, pl.ds(row, half)] = square.T.astype(by_column.dtype)


def choose_kernel(place, kept, across, kept_turned, across_turned, own, lent, turned):
    for colour, rows, columns in ((0, kept, kept_turned), (1, across, across_turned)):

        @pl.when(place[2] == colour)
        def _(rows=rows, columns=columns):
            own[...] = rows[0]
            lent[...] = rows[1]
            turned[...] = columns[...]


def add_kernel(place, own, lent, turned, out, held, copies):
    started = []
    for number, (rows, slot) in enumerate(((own, place[1]), (lent, 1 - place[1]))):
        held[number] = rows[...] + turned[number].astype(held.dtype)
        started += write_rows(held.at[number], out.at[slot], held.at[number], copies.at[number])
    for copy in started:
        copy.wait()


def place_kernel(table, plan, model, scale_table, kind, index, place, scales):
    first, second = plan[0, 0], plan[1, 0]
    low, high = jnp.minimum(first, second), jnp.maximum(first, second)
    found = jnp.right_shift((high - 1) * (high - 2), 1) + low - 1
    picked = [jnp.int32(0)] * len(table[0])
    for number, row in enumerate(table):
        picked = [
            jnp.where(found == number, jnp.int32(value), held) for value, held in zip(row, picked)
        ]
    vector, way, branch, by_colour, turned_over, by_core = picked
    marked = jnp.bitwise_and(lax.axis_index("ex"), vector)
    core = lax.axis_index("layer")
    colour = jnp.bitwise_and(core, by_core)
    for bit in range(max(row[0] for row in table).bit_length()):
        colour = jnp.bitwise_xor(colour, jnp.bitwise_and(jnp.right_shift(marked, bit), 1))
    slot = jnp.bitwise_xor(jnp.bitwise_and(colour, by_colour), turned_over)
    kind[0] = way
    index[0] = branch
    place[0] = core
    place[1] = jnp.where(first > second, 1 - slot, slot)
    place[2] = colour
    for module in range(model.shape[0]):
        scales[module : module + 1, :] = scale_table[pl.ds(model[module], 1), :]


def placed(table, plan, model, scale_table):
    return pl.pallas_call(
        functools.partial(place_kernel, table),
        in_specs=[SMEM, SMEM, VMEM],
        out_specs=[SMEM, SMEM, SMEM, VMEM],
        out_shape=[
            jax.ShapeDtypeStruct((1,), jnp.int32),
            jax.ShapeDtypeStruct((1,), jnp.int32),
            jax.ShapeDtypeStruct((3,), jnp.int32),
            jax.ShapeDtypeStruct((model.shape[0], scale_table.shape[1]), jnp.float32),
        ],
        name="place",
    )(plan, model, scale_table)


def permuted(operand, route):
    return lax.ppermute(operand, "ex", route)


def apart(plans, index, place, payload, scales):
    half = payload.shape[2] // 2
    received = lax.switch(
        index, [lambda held, feed=feed: permuted(held, feed) for feed, _ in plans], payload
    )
    kept, passed = on_device(
        tile_kernel,
        [((half, 2 * half), jnp.float32), ((half, 3 * half), jnp.float32)],
        place,
        payload,
        scales,
        received,
    )
    across = lax.ppermute(passed, "layer", SWAP)
    own, turned = on_device(
        join_kernel,
        [((half, 2 * half), jnp.float32), ((half, 2 * half), jnp.bfloat16)],
        place,
        kept,
        passed,
        across,
    )
    reply = lax.switch(
        index, [lambda held, reply=reply: permuted(held, reply) for _, reply in plans], turned
    )
    return settled(fill_kernel, place, own, reply)


def crossed_routes(mask, between, vector, count):
    feed = [(block, block ^ mask) for block in range(count) if parity(block & vector)]
    lend = [(block, block ^ between) for block in range(count) if not parity(block & vector)]
    reply = [(block, block ^ mask) for block in range(count) if not parity(block & vector)]
    return feed, lend, reply


def together(plans, index, place, payload, scales):
    half = payload.shape[2] // 2
    lent, received = lax.switch(
        index,
        [
            lambda held, feed=feed, lend=lend: (permuted(held, lend), permuted(held, feed))
            for feed, lend, _ in plans
        ],
        payload,
    )
    kept, passed = on_device(
        two_tiles_kernel,
        [((2, half, 2 * half), jnp.float32), ((2, half, 3 * half), jnp.float32)],
        place,
        payload,
        lent,
        scales,
        received,
    )
    across = lax.ppermute(passed, "layer", SWAP)
    own, rows, turned = on_device(
        join_two_kernel,
        [
            ((half, 2 * half), jnp.float32),
            ((half, 2 * half), jnp.bfloat16),
            ((2, half, 2 * half), jnp.bfloat16),
        ],
        place,
        kept,
        passed,
        across,
    )
    rows, turned = lax.switch(
        index,
        [
            lambda held, rows, lend=lend, reply=reply: (permuted(rows, lend), permuted(held, reply))
            for _, lend, reply in plans
        ],
        turned,
        rows,
    )
    return settled(settle_kernel, place, own, rows, turned)


def split_routes(mask, between, vector, count):
    feed, lend = [], []
    for block in range(count):
        for core in range(2):
            lends = parity(block & vector) == core
            end = block ^ (between if lends else mask)
            (lend if lends else feed).append((block * 2 + core, end * 2 + core))
    reply, back = ([(block, block ^ way) for block in range(count)] for way in (mask, between))
    return feed, lend, reply, back


def split(plans, index, place, payload, scales):
    half = payload.shape[2] // 2
    axes = ("ex", "layer")
    lent, received = lax.switch(
        index,
        [
            lambda held, feed=feed, lend=lend: (
                lax.ppermute(held, axes, lend),
                lax.ppermute(held, axes, feed),
            )
            for feed, lend, _, _ in plans
        ],
        payload,
    )
    shape = (2, half, 2 * half)
    kept, passed, kept_turned, passed_turned = on_device(
        quarters_kernel,
        [(shape, jnp.float32)] * 2 + [(shape, jnp.bfloat16)] * 2,
        place,
        payload,
        lent,
        scales,
        received,
    )
    across = lax.ppermute(passed, "layer", SWAP)
    across_turned = lax.ppermute(passed_turned, "layer", SWAP)
    own, rows, turned = on_device(
        choose_kernel,
        [(shape[1:], jnp.float32)] * 2 + [(shape, jnp.bfloat16)],
        place,
        kept,
        across,
        kept_turned,
        across_turned,
    )
    rows, turned = lax.switch(
        index,
        [
            lambda held, rows, reply=reply, back=back: (permuted(rows, back), permuted(held, reply))
            for _, _, reply, back in plans
        ],
        turned,
        rows,
    )
    return settled(add_kernel, place, own, rows, turned)


def paired_rounds(payload, scale_table, plan, model):
    count = lax.axis_size("ex")
    top = count // 2
    apart_plans, together_plans, split_plans, table = [], [], [], []
    for high in range(2, count):
        for low in range(1, high):
            shared = low & high
            if shared == 0 or high >= top > low:
                vector = colouring(low, high, count)
                table.append((vector, 0, len(apart_plans), 1, 1, 0))
                apart_plans.append(routes(low, high, count))
                continue
            mask = low if high < top or not low & 1 else high
            turned_over = int(mask == high)
            if low >= top and (low ^ high) & 1:
                vector = next(
                    choice
                    for choice in range(count - 1, 0, -1)
                    if parity(choice & low) and parity(choice & high) and choice & 2
                )
                table.append((vector, 1, len(together_plans), 0, turned_over, 0))
                together_plans.append(crossed_routes(mask, low ^ high, vector, count))
            else:
                side = top if low >= top else 1 << shared.bit_length() - 1
                table.append((side, 2, len(split_plans), 0, turned_over, 1))
                split_plans.append(split_routes(mask, low ^ high, side, count))
    kind, index, place, scales = placed(table, plan, model, scale_table)
    ways = ((apart, apart_plans), (together, together_plans), (split, split_plans))
    return lax.switch(
        kind[0],
        [functools.partial(way, plans) for way, plans in ways],
        index[0],
        place,
        payload,
        scales,
    )


def direct_rounds(payload, scales, plan):
    count = lax.axis_size("ex")
    own_scaled = (payload[1].astype(jnp.float32) * scales[:, None, :]).astype(jnp.bfloat16)
    outputs = []
    for round_index in range(plan.shape[0]):
        branches = [
            lambda held, mask=mask: lax.ppermute(
                held, "ex", [(block, block ^ mask) for block in range(count)]
            )
            for mask in range(1, count)
        ]
        received = lax.switch(plan[round_index, 0] - 1, branches, payload)
        tile = gram_sum(payload[0], own_scaled, received)
        outputs.append(lax.psum_scatter(tile, "layer", scatter_dimension=0, tiled=True))
    return jnp.stack(outputs)


def shards(acts, grads, adam_scale, plan, assignment):
    payload = jnp.stack([module_major(acts), module_major(grads)])
    if lax.axis_size("ex") > MOST_BLOCKS:
        return direct_rounds(payload, adam_scale[assignment], plan)
    return paired_rounds(payload, adam_scale, plan, assignment)


def solution(mesh):
    in_specs = (
        P(("grp", "ex"), "layer", None),
        P(("grp", "ex"), "layer", None),
        P("grp", None),
        P(),
        P("layer"),
    )
    out_specs = P(None, ("grp", "ex", "layer"), None)
    return jax.shard_map(shards, mesh=mesh, in_specs=in_specs, out_specs=out_specs, check_vma=False)
```

```python
import functools

import jax
import jax.numpy as jnp
from jax import lax
from jax.experimental import pallas as pl
from jax.experimental.pallas import tpu as pltpu
from jax.sharding import PartitionSpec as P

MOST_BLOCKS = 8
TRANSPOSED = (((1,), (1,)), ((), ()))
VMEM = pl.BlockSpec(memory_space=pltpu.VMEM)
SMEM = pl.BlockSpec(memory_space=pltpu.SMEM)
PIECES = 2
SWAP = [(0, 1), (1, 0)]
ROOMY = pltpu.CompilerParams(vmem_limit_bytes=32 * 2**20)


def parity(number):
    return bin(number).count("1") & 1


def module_major(rows):
    return jnp.transpose(rows, (1, 0, 2))


def gram_sum(own_acts, own_scaled, partner):
    act_gram = jnp.einsum("mip,mjp->mij", own_acts, partner[0], preferred_element_type=jnp.float32)
    grad_gram = jnp.einsum("mip,mjp->mij", own_scaled, partner[1], preferred_element_type=jnp.float32)
    return jnp.sum(act_gram * grad_gram, axis=0)


def busiest(low, high, vector, count):
    load = {}
    for block in range(count):
        end = block ^ (high if parity(block & vector) else low)
        at, to = block >> 1, end >> 1
        step = 1 if to > at else -1
        while at != to:
            load[at, block & 1, step] = load.get((at, block & 1, step), 0) + 1
            at += step
        if (block ^ end) & 1:
            load[to, block & 1, 0] = load.get((to, block & 1, 0), 0) + 1
    return max(load.values())


def colouring(low, high, count):
    found = [vector for vector in range(1, count) if parity(vector & low) and parity(vector & high)]
    return min(found, key=lambda vector: busiest(low, high, vector, count))


def routes(low, high, count):
    vector = colouring(low, high, count)
    feed, reply = [], []
    for block in range(count):
        own, other = (low, high) if parity(block & vector) else (high, low)
        feed.append((block, block ^ other))
        reply.append((block, block ^ own))
    return feed, reply


def grams(own, scales, partner, row, column, size):
    total = None
    for module in range(own.shape[1]):
        rows, columns = pl.ds(row, size), pl.ds(column, size)
        act = lax.dot_general(
            own[0, module, rows, :],
            partner[0, module, columns, :],
            TRANSPOSED,
            preferred_element_type=jnp.float32,
        )
        scaled = (
            own[1, module, rows, :].astype(jnp.float32) * scales[module : module + 1, :]
        ).astype(jnp.bfloat16)
        grad = lax.dot_general(
            scaled, partner[1, module, columns, :], TRANSPOSED, preferred_element_type=jnp.float32
        )
        total = act * grad if total is None else total + act * grad
    return total


def parts_of(core, half):
    return pl.multiple_of(core * half, half), pl.multiple_of((1 - core) * half, half)


def tile_halves(core, own, scales, partner, kept, passed):
    half, wide = kept.shape
    mine, theirs = parts_of(core, half)
    for column in range(0, wide, half):
        passed[:, column : column + half] = grams(own, scales, partner, theirs, column, half)
        kept[:, column : column + half] = grams(own, scales, partner, mine, column, half)
    passed[:, wide:] = kept[:, pl.ds(theirs, half)]


def tile_kernel(place, own, scales, partner, kept, passed):
    tile_halves(place[0], own, scales, partner, kept, passed)


def two_tiles_kernel(place, own, lent, scales, partner, kept, passed):
    @pl.when(place[2] == 0)
    def _():
        tile_halves(place[0], own, scales, partner, kept.at[0], passed.at[0])
        tile_halves(place[0], lent, scales, partner, kept.at[1], passed.at[1])


def on_device(kernel, shapes, *operands):
    return pl.pallas_call(
        kernel,
        in_specs=[SMEM if operand.ndim == 1 else VMEM for operand in operands],
        out_specs=[VMEM] * len(shapes),
        out_shape=[jax.ShapeDtypeStruct(shape, dtype) for shape, dtype in shapes],
        compiler_params=ROOMY,
        name=kernel.__name__,
    )(*operands)


def join_kernel(place, kept, passed, across, own, turned):
    core = place[0]
    half, wide = kept.shape
    mine = pl.ds(pl.multiple_of(core * half, half), half)
    theirs = pl.ds(pl.multiple_of((1 - core) * half, half), half)
    own[...] = kept[...] + across[:, :wide]
    turned[:, mine] = own[:, mine].T.astype(turned.dtype)
    turned[:, theirs] = (passed[:, mine] + across[:, wide:]).T.astype(turned.dtype)


def write_rows(source, target, held, copies):
    pieces = copies.shape[0]
    size = source.shape[0] // pieces
    started = []
    for piece in range(pieces):
        rows = pl.ds(piece * size, size)
        if source.dtype != held.dtype:
            held[rows, :] = source[rows, :].astype(held.dtype)
        copy = pltpu.make_async_copy(
            (source if source.dtype == held.dtype else held).at[rows, :],
            target.at[rows, :],
            copies.at[piece],
        )
        copy.start()
        started.append(copy)
    return started


def fill_kernel(place, own, reply, out, held, copies):
    started = write_rows(own, out.at[place[1]], held.at[0], copies.at[0])
    started += write_rows(reply, out.at[1 - place[1]], held.at[1], copies.at[1])
    for copy in started:
        copy.wait()


def settle_kernel(place, own, lent, turned, out, held, copies):
    @pl.when(place[2] == 0)
    def _():
        fill_kernel(place, own, lent, out, held, copies)

    @pl.when(place[2] == 1)
    def _():
        fill_kernel(place, turned.at[0], turned.at[1], out, held, copies)


def settled(kernel, place, *operands):
    half, wide = operands[0].shape
    return pl.pallas_call(
        kernel,
        in_specs=[SMEM] + [VMEM] * len(operands),
        out_specs=pl.BlockSpec(memory_space=pltpu.HBM),
        out_shape=pltpu.HBM((2, half, wide), jnp.float32),
        scratch_shapes=[
            pltpu.VMEM((2, half, wide), jnp.float32),
            pltpu.SemaphoreType.DMA((2, PIECES)),
        ],
        compiler_params=ROOMY,
        name=kernel.__name__,
    )(place, *operands)


def join_two_kernel(place, kept, passed, across, own, lent, turned):
    @pl.when(place[2] == 0)
    def _():
        core = place[0]
        half, wide = own.shape
        mine = pl.ds(pl.multiple_of(core * half, half), half)
        theirs = pl.ds(pl.multiple_of((1 - core) * half, half), half)
        own[...] = kept[0] + across[0, :, :wide]
        lent[...] = (kept[1] + across[1, :, :wide]).astype(lent.dtype)
        for number in range(2):
            turned[number, :, mine] = (
                (kept[number, :, mine] + across[number, :, mine]).T.astype(turned.dtype)
            )
            turned[number, :, theirs] = (
                (passed[number, :, mine] + across[number, :, wide:]).T.astype(turned.dtype)
            )


def quarters_kernel(place, own, lent, scales, partner, kept, passed, kept_turned, passed_turned):
    @pl.when(place[2] == 0)
    def _():
        half = kept.shape[1]
        mine, theirs = parts_of(place[0], half)
        for number, rows in enumerate((own, lent)):
            for row, by_row in ((theirs, passed), (mine, kept)):
                for column, by_column in ((theirs, passed_turned), (mine, kept_turned)):
                    square = grams(rows, scales, partner, row, column, half)
                    by_row[number, :, pl.ds(column, half)] = square
                    by_column[number, :, pl.ds(row, half)] = square.T.astype(by_column.dtype)


def choose_kernel(place, kept, across, kept_turned, across_turned, own, lent, turned):
    for colour, rows, columns in ((0, kept, kept_turned), (1, across, across_turned)):

        @pl.when(place[2] == colour)
        def _(rows=rows, columns=columns):
            own[...] = rows[0]
            lent[...] = rows[1].astype(lent.dtype)
            turned[...] = columns[...]


def add_kernel(place, own, lent, turned, out, held, copies):
    started = []
    for number, (rows, slot) in enumerate(((own, place[1]), (lent, 1 - place[1]))):
        held[number] = rows[...].astype(held.dtype) + turned[number].astype(held.dtype)
        started += write_rows(held.at[number], out.at[slot], held.at[number], copies.at[number])
    for copy in started:
        copy.wait()


def place_kernel(table, plan, model, scale_table, kind, index, place, scales):
    first, second = plan[0, 0], plan[1, 0]
    low, high = jnp.minimum(first, second), jnp.maximum(first, second)
    found = jnp.right_shift((high - 1) * (high - 2), 1) + low - 1
    picked = [jnp.int32(0)] * len(table[0])
    for number, row in enumerate(table):
        picked = [
            jnp.where(found == number, jnp.int32(value), held) for value, held in zip(row, picked)
        ]
    vector, way, branch, by_colour, turned_over, by_core = picked
    marked = jnp.bitwise_and(lax.axis_index("ex"), vector)
    core = lax.axis_index("layer")
    colour = jnp.bitwise_and(core, by_core)
    for bit in range(max(row[0] for row in table).bit_length()):
        colour = jnp.bitwise_xor(colour, jnp.bitwise_and(jnp.right_shift(marked, bit), 1))
    slot = jnp.bitwise_xor(jnp.bitwise_and(colour, by_colour), turned_over)
    kind[0] = way
    index[0] = branch
    place[0] = core
    place[1] = jnp.where(first > second, 1 - slot, slot)
    place[2] = colour
    for module in range(model.shape[0]):
        scales[module : module + 1, :] = scale_table[pl.ds(model[module], 1), :]


def placed(table, plan, model, scale_table):
    return pl.pallas_call(
        functools.partial(place_kernel, table),
        in_specs=[SMEM, SMEM, VMEM],
        out_specs=[SMEM, SMEM, SMEM, VMEM],
        out_shape=[
            jax.ShapeDtypeStruct((1,), jnp.int32),
            jax.ShapeDtypeStruct((1,), jnp.int32),
            jax.ShapeDtypeStruct((3,), jnp.int32),
            jax.ShapeDtypeStruct((model.shape[0], scale_table.shape[1]), jnp.float32),
        ],
        name="place",
    )(plan, model, scale_table)


def permuted(operand, route):
    return lax.ppermute(operand, "ex", route)


def apart(plans, index, place, payload, scales):
    half = payload.shape[2] // 2
    received = lax.switch(
        index, [lambda held, feed=feed: permuted(held, feed) for feed, _ in plans], payload
    )
    kept, passed = on_device(
        tile_kernel,
        [((half, 2 * half), jnp.float32), ((half, 3 * half), jnp.float32)],
        place,
        payload,
        scales,
        received,
    )
    across = lax.ppermute(passed, "layer", SWAP)
    own, turned = on_device(
        join_kernel,
        [((half, 2 * half), jnp.float32), ((half, 2 * half), jnp.bfloat16)],
        place,
        kept,
        passed,
        across,
    )
    reply = lax.switch(
        index, [lambda held, reply=reply: permuted(held, reply) for _, reply in plans], turned
    )
    return settled(fill_kernel, place, own, reply)


def crossed_routes(mask, between, vector, count):
    feed = [(block, block ^ mask) for block in range(count) if parity(block & vector)]
    lend = [(block, block ^ between) for block in range(count) if not parity(block & vector)]
    reply = [(block, block ^ mask) for block in range(count) if not parity(block & vector)]
    return feed, lend, reply


def together(plans, index, place, payload, scales):
    half = payload.shape[2] // 2
    lent, received = lax.switch(
        index,
        [
            lambda held, feed=feed, lend=lend: (permuted(held, lend), permuted(held, feed))
            for feed, lend, _ in plans
        ],
        payload,
    )
    kept, passed = on_device(
        two_tiles_kernel,
        [((2, half, 2 * half), jnp.float32), ((2, half, 3 * half), jnp.float32)],
        place,
        payload,
        lent,
        scales,
        received,
    )
    across = lax.ppermute(passed, "layer", SWAP)
    own, rows, turned = on_device(
        join_two_kernel,
        [
            ((half, 2 * half), jnp.float32),
            ((half, 2 * half), jnp.bfloat16),
            ((2, half, 2 * half), jnp.bfloat16),
        ],
        place,
        kept,
        passed,
        across,
    )
    rows, turned = lax.switch(
        index,
        [
            lambda held, rows, lend=lend, reply=reply: (permuted(rows, lend), permuted(held, reply))
            for _, lend, reply in plans
        ],
        turned,
        rows,
    )
    return settled(settle_kernel, place, own, rows, turned)


def split_routes(mask, between, vector, count):
    feed, lend = [], []
    for block in range(count):
        for core in range(2):
            lends = parity(block & vector) == core
            end = block ^ (between if lends else mask)
            (lend if lends else feed).append((block * 2 + core, end * 2 + core))
    reply, back = ([(block, block ^ way) for block in range(count)] for way in (mask, between))
    return feed, lend, reply, back


def split(plans, index, place, payload, scales):
    half = payload.shape[2] // 2
    axes = ("ex", "layer")
    lent, received = lax.switch(
        index,
        [
            lambda held, feed=feed, lend=lend: (
                lax.ppermute(held, axes, lend),
                lax.ppermute(held, axes, feed),
            )
            for feed, lend, _, _ in plans
        ],
        payload,
    )
    shape = (2, half, 2 * half)
    kept, passed, kept_turned, passed_turned = on_device(
        quarters_kernel,
        [(shape, jnp.float32)] * 2 + [(shape, jnp.bfloat16)] * 2,
        place,
        payload,
        lent,
        scales,
        received,
    )
    across = lax.ppermute(passed, "layer", SWAP)
    across_turned = lax.ppermute(passed_turned, "layer", SWAP)
    own, rows, turned = on_device(
        choose_kernel,
        [(shape[1:], jnp.float32), (shape[1:], jnp.bfloat16), (shape, jnp.bfloat16)],
        place,
        kept,
        across,
        kept_turned,
        across_turned,
    )
    rows, turned = lax.switch(
        index,
        [
            lambda held, rows, reply=reply, back=back: (permuted(rows, back), permuted(held, reply))
            for _, _, reply, back in plans
        ],
        turned,
        rows,
    )
    return settled(add_kernel, place, own, rows, turned)


def paired_rounds(payload, scale_table, plan, model):
    count = lax.axis_size("ex")
    top = count // 2
    apart_plans, together_plans, split_plans, table = [], [], [], []
    for high in range(2, count):
        for low in range(1, high):
            shared = low & high
            if shared == 0 or high >= top > low:
                vector = colouring(low, high, count)
                table.append((vector, 0, len(apart_plans), 1, 1, 0))
                apart_plans.append(routes(low, high, count))
                continue
            mask = low if high < top or not low & 1 else high
            turned_over = int(mask == high)
            if low >= top and (low ^ high) & 1:
                vector = next(
                    choice
                    for choice in range(count - 1, 0, -1)
                    if parity(choice & low) and parity(choice & high) and choice & 2
                )
                table.append((vector, 1, len(together_plans), 0, turned_over, 0))
                together_plans.append(crossed_routes(mask, low ^ high, vector, count))
            else:
                side = top if low >= top else 1 << shared.bit_length() - 1
                table.append((side, 2, len(split_plans), 0, turned_over, 1))
                split_plans.append(split_routes(mask, low ^ high, side, count))
    kind, index, place, scales = placed(table, plan, model, scale_table)
    ways = ((apart, apart_plans), (together, together_plans), (split, split_plans))
    return lax.switch(
        kind[0],
        [functools.partial(way, plans) for way, plans in ways],
        index[0],
        place,
        payload,
        scales,
    )


def direct_rounds(payload, scales, plan):
    count = lax.axis_size("ex")
    own_scaled = (payload[1].astype(jnp.float32) * scales[:, None, :]).astype(jnp.bfloat16)
    outputs = []
    for round_index in range(plan.shape[0]):
        branches = [
            lambda held, mask=mask: lax.ppermute(
                held, "ex", [(block, block ^ mask) for block in range(count)]
            )
            for mask in range(1, count)
        ]
        received = lax.switch(plan[round_index, 0] - 1, branches, payload)
        tile = gram_sum(payload[0], own_scaled, received)
        outputs.append(lax.psum_scatter(tile, "layer", scatter_dimension=0, tiled=True))
    return jnp.stack(outputs)


def shards(acts, grads, adam_scale, plan, assignment):
    payload = jnp.stack([module_major(acts), module_major(grads)])
    if lax.axis_size("ex") > MOST_BLOCKS:
        return direct_rounds(payload, adam_scale[assignment], plan)
    return paired_rounds(payload, adam_scale, plan, assignment)


def solution(mesh):
    in_specs = (
        P(("grp", "ex"), "layer", None),
        P(("grp", "ex"), "layer", None),
        P("grp", None),
        P(),
        P("layer"),
    )
    out_specs = P(None, ("grp", "ex", "layer"), None)
    return jax.shard_map(shards, mesh=mesh, in_specs=in_specs, out_specs=out_specs, check_vma=False)
```

```python
import functools

import jax
import jax.numpy as jnp
from jax import lax
from jax.experimental import pallas as pl
from jax.experimental.pallas import tpu as pltpu
from jax.sharding import PartitionSpec as P

MOST_BLOCKS = 8
TRANSPOSED = (((1,), (1,)), ((), ()))
VMEM = pl.BlockSpec(memory_space=pltpu.VMEM)
SMEM = pl.BlockSpec(memory_space=pltpu.SMEM)
PIECES = 2
SWAP = [(0, 1), (1, 0)]
ROOMY = pltpu.CompilerParams(vmem_limit_bytes=32 * 2**20)


def parity(number):
    return bin(number).count("1") & 1


def module_major(rows):
    return jnp.transpose(rows, (1, 0, 2))


def gram_sum(own_acts, own_scaled, partner):
    act_gram = jnp.einsum("mip,mjp->mij", own_acts, partner[0], preferred_element_type=jnp.float32)
    grad_gram = jnp.einsum("mip,mjp->mij", own_scaled, partner[1], preferred_element_type=jnp.float32)
    return jnp.sum(act_gram * grad_gram, axis=0)


def busiest(low, high, vector, count):
    load = {}
    for block in range(count):
        end = block ^ (high if parity(block & vector) else low)
        at, to = block >> 1, end >> 1
        step = 1 if to > at else -1
        while at != to:
            load[at, block & 1, step] = load.get((at, block & 1, step), 0) + 1
            at += step
        if (block ^ end) & 1:
            load[to, block & 1, 0] = load.get((to, block & 1, 0), 0) + 1
    return max(load.values())


def colouring(low, high, count):
    found = [vector for vector in range(1, count) if parity(vector & low) and parity(vector & high)]
    return min(found, key=lambda vector: busiest(low, high, vector, count))


def routes(low, high, count):
    vector = colouring(low, high, count)
    feed, reply = [], []
    for block in range(count):
        own, other = (low, high) if parity(block & vector) else (high, low)
        feed.append((block, block ^ other))
        reply.append((block, block ^ own))
    return feed, reply


def grams(own, scales, partner, row, column, size):
    total = None
    for module in range(own.shape[1]):
        rows, columns = pl.ds(row, size), pl.ds(column, size)
        act = lax.dot_general(
            own[0, module, rows, :],
            partner[0, module, columns, :],
            TRANSPOSED,
            preferred_element_type=jnp.float32,
        )
        scaled = (
            own[1, module, rows, :].astype(jnp.float32) * scales[module : module + 1, :]
        ).astype(jnp.bfloat16)
        grad = lax.dot_general(
            scaled, partner[1, module, columns, :], TRANSPOSED, preferred_element_type=jnp.float32
        )
        total = act * grad if total is None else total + act * grad
    return total


def parts_of(core, half):
    return pl.multiple_of(core * half, half), pl.multiple_of((1 - core) * half, half)


def tile_halves(core, own, scales, partner, kept, passed):
    half, wide = kept.shape
    mine, theirs = parts_of(core, half)
    for column in range(0, wide, half):
        passed[:, column : column + half] = grams(own, scales, partner, theirs, column, half)
        kept[:, column : column + half] = grams(own, scales, partner, mine, column, half)
    passed[:, wide:] = kept[:, pl.ds(theirs, half)]


def tile_kernel(place, own, scales, partner, kept, passed):
    tile_halves(place[0], own, scales, partner, kept, passed)


def two_tiles_kernel(place, own, lent, scales, partner, kept, passed):
    @pl.when(place[2] == 0)
    def _():
        tile_halves(place[0], own, scales, partner, kept.at[0], passed.at[0])
        tile_halves(place[0], lent, scales, partner, kept.at[1], passed.at[1])


def on_device(kernel, shapes, *operands):
    return pl.pallas_call(
        kernel,
        in_specs=[SMEM if operand.ndim == 1 else VMEM for operand in operands],
        out_specs=[VMEM] * len(shapes),
        out_shape=[jax.ShapeDtypeStruct(shape, dtype) for shape, dtype in shapes],
        compiler_params=ROOMY,
        name=kernel.__name__,
    )(*operands)


def join_kernel(place, kept, passed, across, own, turned):
    core = place[0]
    half, wide = kept.shape
    mine = pl.ds(pl.multiple_of(core * half, half), half)
    theirs = pl.ds(pl.multiple_of((1 - core) * half, half), half)
    own[...] = kept[...] + across[:, :wide]
    turned[:, mine] = own[:, mine].T.astype(turned.dtype)
    turned[:, theirs] = (passed[:, mine] + across[:, wide:]).T.astype(turned.dtype)


def write_rows(source, target, held, copies):
    pieces = copies.shape[0]
    size = source.shape[0] // pieces
    started = []
    for piece in range(pieces):
        rows = pl.ds(piece * size, size)
        if source.dtype != held.dtype:
            held[rows, :] = source[rows, :].astype(held.dtype)
        copy = pltpu.make_async_copy(
            (source if source.dtype == held.dtype else held).at[rows, :],
            target.at[rows, :],
            copies.at[piece],
        )
        copy.start()
        started.append(copy)
    return started


def fill_kernel(place, own, reply, out, held, copies):
    started = write_rows(own, out.at[place[1]], held.at[0], copies.at[0])
    started += write_rows(reply, out.at[1 - place[1]], held.at[1], copies.at[1])
    for copy in started:
        copy.wait()


def settle_kernel(place, own, lent, turned, out, held, copies):
    @pl.when(place[2] == 0)
    def _():
        fill_kernel(place, own, lent, out, held, copies)

    @pl.when(place[2] == 1)
    def _():
        fill_kernel(place, turned.at[0], turned.at[1], out, held, copies)


def settled(kernel, place, *operands):
    half, wide = operands[0].shape
    return pl.pallas_call(
        kernel,
        in_specs=[SMEM] + [VMEM] * len(operands),
        out_specs=pl.BlockSpec(memory_space=pltpu.HBM),
        out_shape=pltpu.HBM((2, half, wide), jnp.float32),
        scratch_shapes=[
            pltpu.VMEM((2, half, wide), jnp.float32),
            pltpu.SemaphoreType.DMA((2, PIECES)),
        ],
        compiler_params=ROOMY,
        name=kernel.__name__,
    )(place, *operands)


def join_two_kernel(place, kept, passed, across, own, lent, turned):
    @pl.when(place[2] == 0)
    def _():
        core = place[0]
        half, wide = own.shape
        mine = pl.ds(pl.multiple_of(core * half, half), half)
        theirs = pl.ds(pl.multiple_of((1 - core) * half, half), half)
        own[...] = kept[0] + across[0, :, :wide]
        lent[...] = (kept[1] + across[1, :, :wide]).astype(lent.dtype)
        for number in range(2):
            turned[number, :, mine] = (
                (kept[number, :, mine] + across[number, :, mine]).T.astype(turned.dtype)
            )
            turned[number, :, theirs] = (
                (passed[number, :, mine] + across[number, :, wide:]).T.astype(turned.dtype)
            )


def quarters_kernel(place, own, lent, scales, partner, kept, passed, kept_turned, passed_turned):
    @pl.when(place[2] == 0)
    def _():
        half = kept.shape[1]
        mine, theirs = parts_of(place[0], half)
        for number, rows in enumerate((own, lent)):
            for row, by_row in ((theirs, passed), (mine, kept)):
                for column, by_column in ((theirs, passed_turned), (mine, kept_turned)):
                    square = grams(rows, scales, partner, row, column, half)
                    by_row[number, :, pl.ds(column, half)] = square
                    by_column[number, :, pl.ds(row, half)] = square.T.astype(by_column.dtype)


def choose_kernel(place, kept, across, kept_turned, across_turned, own, lent, turned):
    for colour, rows, columns in ((0, kept, kept_turned), (1, across, across_turned)):

        @pl.when(place[2] == colour)
        def _(rows=rows, columns=columns):
            own[...] = rows[0]
            lent[...] = rows[1].astype(lent.dtype)
            turned[...] = columns[...]


def add_kernel(place, own, lent, turned, out, held, copies):
    started = []
    for number, (rows, slot) in enumerate(((own, place[1]), (lent, 1 - place[1]))):
        held[number] = rows[...].astype(held.dtype) + turned[number].astype(held.dtype)
        started += write_rows(held.at[number], out.at[slot], held.at[number], copies.at[number])
    for copy in started:
        copy.wait()


def place_kernel(table, plan, model, scale_table, kind, index, place, scales):
    first, second = plan[0, 0], plan[1, 0]
    low, high = jnp.minimum(first, second), jnp.maximum(first, second)
    found = jnp.right_shift((high - 1) * (high - 2), 1) + low - 1
    picked = [jnp.int32(0)] * len(table[0])
    for number, row in enumerate(table):
        picked = [
            jnp.where(found == number, jnp.int32(value), held) for value, held in zip(row, picked)
        ]
    vector, way, branch, by_colour, turned_over, by_core = picked
    marked = jnp.bitwise_and(lax.axis_index("ex"), vector)
    core = lax.axis_index("layer")
    colour = jnp.bitwise_and(core, by_core)
    for bit in range(max(row[0] for row in table).bit_length()):
        colour = jnp.bitwise_xor(colour, jnp.bitwise_and(jnp.right_shift(marked, bit), 1))
    slot = jnp.bitwise_xor(jnp.bitwise_and(colour, by_colour), turned_over)
    kind[0] = way
    index[0] = branch
    place[0] = core
    place[1] = jnp.where(first > second, 1 - slot, slot)
    place[2] = colour
    for module in range(model.shape[0]):
        scales[module : module + 1, :] = scale_table[pl.ds(model[module], 1), :]


def placed(table, plan, model, scale_table):
    return pl.pallas_call(
        functools.partial(place_kernel, table),
        in_specs=[SMEM, SMEM, VMEM],
        out_specs=[SMEM, SMEM, SMEM, VMEM],
        out_shape=[
            jax.ShapeDtypeStruct((1,), jnp.int32),
            jax.ShapeDtypeStruct((1,), jnp.int32),
            jax.ShapeDtypeStruct((3,), jnp.int32),
            jax.ShapeDtypeStruct((model.shape[0], scale_table.shape[1]), jnp.float32),
        ],
        name="place",
    )(plan, model, scale_table)


def permuted(operand, route):
    return lax.ppermute(operand, "ex", route)


def apart(plans, index, place, payload, scales):
    half = payload.shape[2] // 2
    received = lax.switch(
        index, [lambda held, feed=feed: permuted(held, feed) for feed, _ in plans], payload
    )
    kept, passed = on_device(
        tile_kernel,
        [((half, 2 * half), jnp.float32), ((half, 3 * half), jnp.float32)],
        place,
        payload,
        scales,
        received,
    )
    across = lax.ppermute(passed, "layer", SWAP)
    own, turned = on_device(
        join_kernel,
        [((half, 2 * half), jnp.float32), ((half, 2 * half), jnp.bfloat16)],
        place,
        kept,
        passed,
        across,
    )
    reply = lax.switch(
        index, [lambda held, reply=reply: permuted(held, reply) for _, reply in plans], turned
    )
    return settled(fill_kernel, place, own, reply)


def crossed_routes(mask, between, vector, count):
    feed = [(block, block ^ mask) for block in range(count) if parity(block & vector)]
    lend = [(block, block ^ between) for block in range(count) if not parity(block & vector)]
    reply = [(block, block ^ mask) for block in range(count) if not parity(block & vector)]
    return feed, lend, reply


def together(plans, index, place, payload, scales):
    half = payload.shape[2] // 2
    lent, received = lax.switch(
        index,
        [
            lambda held, feed=feed, lend=lend: (permuted(held, lend), permuted(held, feed))
            for feed, lend, _ in plans
        ],
        payload,
    )
    kept, passed = on_device(
        two_tiles_kernel,
        [((2, half, 2 * half), jnp.float32), ((2, half, 3 * half), jnp.float32)],
        place,
        payload,
        lent,
        scales,
        received,
    )
    across = lax.ppermute(passed, "layer", SWAP)
    own, rows, turned = on_device(
        join_two_kernel,
        [
            ((half, 2 * half), jnp.float32),
            ((half, 2 * half), jnp.bfloat16),
            ((2, half, 2 * half), jnp.bfloat16),
        ],
        place,
        kept,
        passed,
        across,
    )
    rows, turned = lax.switch(
        index,
        [
            lambda held, rows, lend=lend, reply=reply: (permuted(rows, lend), permuted(held, reply))
            for _, lend, reply in plans
        ],
        turned,
        rows,
    )
    return settled(settle_kernel, place, own, rows, turned)


def split_routes(mask, between, vector, count):
    feed, lend = [], []
    for block in range(count):
        for core in range(2):
            lends = parity(block & vector) == core
            end = block ^ (between if lends else mask)
            (lend if lends else feed).append((block * 2 + core, end * 2 + core))
    reply, back = ([(block, block ^ way) for block in range(count)] for way in (mask, between))
    return feed, lend, reply, back


def split(plans, index, place, payload, scales):
    half = payload.shape[2] // 2
    axes = ("ex", "layer")
    lent, received = lax.switch(
        index,
        [
            lambda held, feed=feed, lend=lend: (
                lax.ppermute(held, axes, lend),
                lax.ppermute(held, axes, feed),
            )
            for feed, lend, _, _ in plans
        ],
        payload,
    )
    shape = (2, half, 2 * half)
    kept, passed, kept_turned, passed_turned = on_device(
        quarters_kernel,
        [(shape, jnp.float32)] * 2 + [(shape, jnp.bfloat16)] * 2,
        place,
        payload,
        lent,
        scales,
        received,
    )
    across = lax.ppermute(passed, "layer", SWAP)
    across_turned = lax.ppermute(passed_turned, "layer", SWAP)
    own, rows, turned = on_device(
        choose_kernel,
        [(shape[1:], jnp.float32), (shape[1:], jnp.bfloat16), (shape, jnp.bfloat16)],
        place,
        kept,
        across,
        kept_turned,
        across_turned,
    )
    rows, turned = lax.switch(
        index,
        [
            lambda held, rows, reply=reply, back=back: (permuted(rows, back), permuted(held, reply))
            for _, _, reply, back in plans
        ],
        turned,
        rows,
    )
    return settled(add_kernel, place, own, rows, turned)


def paired_rounds(payload, scale_table, plan, model):
    count = lax.axis_size("ex")
    top = count // 2
    apart_plans, together_plans, split_plans, table = [], [], [], []
    for high in range(2, count):
        for low in range(1, high):
            shared = low & high
            if shared == 0 or high >= top > low:
                vector = colouring(low, high, count)
                table.append((vector, 0, len(apart_plans), 1, 1, 0))
                apart_plans.append(routes(low, high, count))
                continue
            mask = low if high < top or (low ^ high) & 1 and not low & 1 else high
            turned_over = int(mask == high)
            if low >= top and (low ^ high) & 1:
                vector = next(
                    choice
                    for choice in range(count - 1, 0, -1)
                    if parity(choice & low) and parity(choice & high) and choice & 2
                )
                table.append((vector, 1, len(together_plans), 0, turned_over, 0))
                together_plans.append(crossed_routes(mask, low ^ high, vector, count))
            else:
                side = top if low >= top else 1 << shared.bit_length() - 1
                table.append((side, 2, len(split_plans), 0, turned_over, 1))
                split_plans.append(split_routes(mask, low ^ high, side, count))
    kind, index, place, scales = placed(table, plan, model, scale_table)
    ways = ((apart, apart_plans), (together, together_plans), (split, split_plans))
    return lax.switch(
        kind[0],
        [functools.partial(way, plans) for way, plans in ways],
        index[0],
        place,
        payload,
        scales,
    )


def direct_rounds(payload, scales, plan):
    count = lax.axis_size("ex")
    own_scaled = (payload[1].astype(jnp.float32) * scales[:, None, :]).astype(jnp.bfloat16)
    outputs = []
    for round_index in range(plan.shape[0]):
        branches = [
            lambda held, mask=mask: lax.ppermute(
                held, "ex", [(block, block ^ mask) for block in range(count)]
            )
            for mask in range(1, count)
        ]
        received = lax.switch(plan[round_index, 0] - 1, branches, payload)
        tile = gram_sum(payload[0], own_scaled, received)
        outputs.append(lax.psum_scatter(tile, "layer", scatter_dimension=0, tiled=True))
    return jnp.stack(outputs)


def shards(acts, grads, adam_scale, plan, assignment):
    payload = jnp.stack([module_major(acts), module_major(grads)])
    if lax.axis_size("ex") > MOST_BLOCKS:
        return direct_rounds(payload, adam_scale[assignment], plan)
    return paired_rounds(payload, adam_scale, plan, assignment)


def solution(mesh):
    in_specs = (
        P(("grp", "ex"), "layer", None),
        P(("grp", "ex"), "layer", None),
        P("grp", None),
        P(),
        P("layer"),
    )
    out_specs = P(None, ("grp", "ex", "layer"), None)
    return jax.shard_map(shards, mesh=mesh, in_specs=in_specs, out_specs=out_specs, check_vma=False)
```
